512 devices in a mesh: row: 32 (over y_hi, z, core), col: 16 (over y_lo, x).
Axes of the slice: x: 4, y: 8 (y_hi: 2, y_lo: 4; y = y_hi * 4 + y_lo), z: 8, core: 2. Of those that a mesh axis runs over, the one named last changes fastest.
Arguments:
- features: bfloat16 [128, 96, 1536], P('row', 'col'), may hold values from -6 to 6
- kernel: float32 [49, 1536], replicated, may hold values from -0.875 to 0.875
- ln_gain: float32 [1536], replicated, may hold values from 0.25 to 1.75
- ln_bias: float32 [1536], replicated, may hold values from -3 to 3
- w_up: bfloat16 [1536, 4096], P(None, 'col'), may hold values from -0.15625 to 0.15625
- b_up: float32 [4096], P('col'), may hold values from -3 to 3
- w_down: bfloat16 [4096, 1536], P('col'), may hold values from -0.1875 to 0.1875
- layer_scale: float32 [1536], replicated, may hold values from 0.3 to 1.2
- text_embed: bfloat16 [6144, 1536], P(('row', 'col')), may hold values from -6 to 6
- slot_token: int32 [6144], P(('row', 'col')), may hold values from -1 to 95, as said below
- seq_grad: bfloat16 [6144, 1536], P(('row', 'col')), may hold values from -6 to 6
Outputs:
- seq_embed: bfloat16 [6144, 1536], P(('row', 'col'))
- grad_input: bfloat16 [128, 96, 1536], P('row', 'col')
- grad_kernel: float32 [49, 1536], replicated
- grad_up: bfloat16 [1536, 4096], P(None, 'col')
- grad_down: bfloat16 [4096, 1536], P('col')
The draws below stay inside these ranges and needn't reach their ends.
Inputs may be any that keep to these rules, and one draw needn't show every extreme that they name: `slot_token`: -1 marks a text slot. In each band's slots every image token of the band appears exactly once, in row-major order of the band's tokens; half of the slots hold image tokens.
All inputs are finite; a program needn't handle non-finite values.
Results may differ from the reference program's by a relative error of at most 0.03.
Values may be sent and summed in bfloat16 or wider, within the bound.
A program may use at most 64 MiB of HBM per device.

```python
import jax
import jax.numpy as jnp
from jax import lax

D = 1536
FFW = 4096
ROWS_DEV = 4
COLS_DEV = 6
TOKB = 6
SEQ_DEV = 12
HH = 128
WW = 96
SEQ = 6144
N_ROW = 32
N_COL = 16


def draw_slot_token(key, part):
    key = jax.random.fold_in(key, 7)
    band_slots = N_COL * SEQ_DEV
    band_tokens = N_COL * TOKB
    half_cols = COLS_DEV // 2
    order = jnp.arange(band_tokens, dtype=jnp.int32)
    token_row = order // (N_COL * half_cols)
    token_col = order % (N_COL * half_cols)
    block_index = token_col // half_cols * TOKB + token_row * half_cols + token_col % half_cols

    def one_band(subkey):
        shuffled = jax.random.permutation(subkey, band_slots)
        chosen = jnp.sort(shuffled[:band_tokens])
        return jnp.full((band_slots,), -1, jnp.int32).at[chosen].set(block_index.astype(jnp.int32))
    keys = jax.random.split(key, N_ROW)
    return jax.vmap(one_band)(keys).reshape(-1)


def shard_levels(key, extent, pieces, smallest, largest):
    def one(position, blocks):
        steps = jax.random.uniform(jax.random.fold_in(jax.random.fold_in(key, 6), position), (blocks,), jnp.float32, smallest / len(pieces), largest / len(pieces))
        return jnp.repeat(jnp.exp(steps), extent[position] // blocks).reshape((-1,) + (1,) * (len(extent) - position - 1))

    factor_of = one(*pieces[0])
    for cut in pieces[1:]:
        factor_of = factor_of * one(*cut)
    return factor_of


def gaussian(rng, extent, scale, reach, shards=(), kind=jnp.bfloat16):
    gain = shard_levels(rng, extent, shards, -0.22, 0.18) if shards else 1.0
    entries = jax.random.normal(rng, extent, jnp.float32) * scale * gain
    return jnp.minimum(jnp.maximum(entries, -reach), reach).astype(kind)


def setup_inputs(seed: int = 0) -> dict:
    key_list = jax.random.split(jax.random.key(seed), 12)
    features = gaussian(key_list[0], (HH, WW, D), 1.0, 6.0, ((0, 32), (1, 16)))
    kernel = gaussian(key_list[1], (49, D), 49 ** -0.5, 0.875, (), jnp.float32)
    ln_gain = jnp.clip(1.0 + 0.15 * jax.random.normal(key_list[2], (D,), jnp.float32), 0.25, 1.75)
    ln_bias = gaussian(key_list[3], (D,), 0.5, 3.0, (), jnp.float32)
    w_up = gaussian(key_list[4], (D, FFW), D ** -0.5, 0.15625, ((1, 16),))
    b_up = gaussian(key_list[5], (FFW,), 0.5, 3.0, ((0, 16),), jnp.float32)
    w_down = gaussian(key_list[6], (FFW, D), (FFW // 4) ** -0.5, 0.1875, ((0, 16),))
    layer_scale = jnp.clip(jax.random.uniform(key_list[7], (D,), jnp.float32, 0.3, 1.2), 0.3, 1.2)
    text_embed = gaussian(key_list[8], (SEQ, D), 1.0, 6.0, ((0, 512),))
    slot_token = draw_slot_token(jax.random.fold_in(key_list[11], 71), 0)
    seq_grad = gaussian(key_list[10], (SEQ, D), 1.0, 6.0, ((0, 512),))
    return dict(features=features, kernel=kernel, ln_gain=ln_gain, ln_bias=ln_bias, w_up=w_up, b_up=b_up, w_down=w_down, layer_scale=layer_scale, text_embed=text_embed, slot_token=slot_token, seq_grad=seq_grad)


def layer_norm(mixed, ln_gain, ln_bias):
    mean = lax.optimization_barrier(jnp.mean(mixed, axis=-1, keepdims=True))
    centred = mixed - mean
    var = lax.optimization_barrier(jnp.mean(centred * centred, axis=-1, keepdims=True))
    return centred * lax.rsqrt(var + 1e-06) * ln_gain + ln_bias

def gelu_tanh(value):
    return jax.nn.gelu(value, approximate=True)

def reference(features, kernel, ln_gain, ln_bias, w_up, b_up, w_down, layer_scale, text_embed, slot_token, seq_grad):
    height, width, chans = features.shape
    padded = jnp.pad(features, ((3, 3), (3, 3), (0, 0)))
    mixed = jnp.zeros((height, width, chans), jnp.float32)
    for tap in range(49):
        p, q = (tap // 7, tap % 7)
        mixed = mixed + padded[p:p + height, q:q + width].astype(jnp.float32) * kernel[tap]
    normed = layer_norm(mixed, ln_gain, ln_bias).astype(jnp.bfloat16)
    flat = normed.reshape(height * width, chans)
    half_rows, half_cols = (ROWS_DEV // 2, COLS_DEV // 2)
    seq_rows = seq_grad.reshape(N_ROW, N_COL * SEQ_DEV, chans)
    slots = slot_token.reshape(N_ROW, N_COL * SEQ_DEV)
    safe = jnp.maximum(slots, 0)
    live = (slots >= 0)[:, :, None]
    band_grad = jnp.zeros((N_ROW, N_COL * TOKB, chans), jnp.float32)
    band_idx = jnp.arange(N_ROW, dtype=jnp.int32)[:, None]
    band_grad = band_grad.at[band_idx, safe].add(jnp.where(live, seq_rows.astype(jnp.float32), 0.0))
    token_grad = band_grad.reshape(N_ROW, N_COL, half_rows, half_cols, chans).transpose(0, 2, 1, 3, 4)
    token_grad = token_grad.reshape(height // 2, width // 2, chans)
    out_grad = jnp.repeat(jnp.repeat(token_grad / 4.0, 2, axis=0), 2, axis=1)
    branch_grad = (layer_scale * out_grad).astype(jnp.bfloat16)
    grad_flat = branch_grad.reshape(height * width, chans)
    share = w_up.shape[1] // N_COL
    branch = jnp.zeros((height * width, chans), jnp.float32)
    normed_grad = jnp.zeros((height * width, chans), jnp.float32)
    up_parts = []
    down_parts = []
    for block in range(N_COL):
        w_up_blk = w_up[:, block * share:(block + 1) * share]
        w_down_blk = w_down[block * share:(block + 1) * share]
        pre = jnp.dot(flat, w_up_blk, preferred_element_type=jnp.float32) + b_up[block * share:(block + 1) * share]
        act = gelu_tanh(pre).astype(jnp.bfloat16)
        branch = branch + jnp.dot(act, w_down_blk, preferred_element_type=jnp.float32)
        act_grad = jnp.dot(grad_flat, w_down_blk.T, preferred_element_type=jnp.float32)
        pre_grad = jax.vjp(gelu_tanh, pre)[1](act_grad)[0].astype(jnp.bfloat16)
        down_parts.append(jnp.dot(act.T, grad_flat, preferred_element_type=jnp.float32))
        up_parts.append(jnp.dot(flat.T, pre_grad, preferred_element_type=jnp.float32))
        term = jnp.dot(pre_grad, w_up_blk.T, preferred_element_type=jnp.float32)
        normed_grad = normed_grad + term.astype(jnp.bfloat16).astype(jnp.float32)
    grad_up = jnp.concatenate(up_parts, axis=1).astype(jnp.bfloat16)
    grad_down = jnp.concatenate(down_parts, axis=0).astype(jnp.bfloat16)
    summed = features.astype(jnp.float32) + layer_scale * branch.reshape(height, width, chans)
    tokens = summed.reshape(height // 2, 2, width // 2, 2, chans).mean(axis=(1, 3)).astype(jnp.bfloat16)
    band_tokens = tokens.reshape(N_ROW, half_rows, N_COL, half_cols, chans).transpose(0, 2, 1, 3, 4)
    band_tokens = band_tokens.reshape(N_ROW, N_COL * TOKB, chans)
    picked = jnp.take_along_axis(band_tokens, safe[:, :, None], axis=1)
    text_rows = text_embed.reshape(N_ROW, N_COL * SEQ_DEV, chans)
    seq_embed = jnp.where(live, picked, text_rows).reshape(SEQ, chans)
    norm_vjp = jax.vjp(lambda m: layer_norm(m, ln_gain, ln_bias), mixed)[1]
    mixed_grad = norm_vjp(normed_grad.reshape(height, width, chans))[0].astype(jnp.bfloat16)
    grad_padded = jnp.pad(mixed_grad, ((3, 3), (3, 3), (0, 0)))
    input_grad = out_grad
    kernel_rows = []
    for tap in range(49):
        p, q = (tap // 7, tap % 7)
        input_grad = input_grad + grad_padded[6 - p:6 - p + height, 6 - q:6 - q + width].astype(jnp.float32) * kernel[tap]
        kernel_rows.append(lax.optimization_barrier(jnp.sum(padded[p:p + height, q:q + width].astype(jnp.float32) * mixed_grad.astype(jnp.float32), axis=(0, 1))))
    grad_kernel = jnp.stack(kernel_rows, axis=0)
    return (seq_embed, input_grad.astype(jnp.bfloat16), grad_kernel, grad_up, grad_down)
```

```python
import functools

import jax
import jax.numpy as jnp
import numpy as np
from jax import lax
from jax.experimental import pallas as pl
from jax.experimental.pallas import tpu as pltpu
from jax.sharding import PartitionSpec as P

F32, BF16 = jnp.float32, jnp.bfloat16
D, LANE, SUB = 1536, 128, 12
ROWS, COLS, PIX, SLOTS, SLOT_PAD = 4, 6, 24, 12, 16
N_ROW, N_COL = 32, 16
NX, NY = 4, 4
NZ, NC = 8, 2
HID = 256
DIRS = [(a, b) for a in (-1, 0, 1) for b in (-1, 0, 1) if (a, b) != (0, 0)]
MESH = pl.DeviceIdType.MESH
VMEM_LIMIT = 48 * 1024 * 1024
SRC_ROW = {1: (1, 3), 0: (0, 4), -1: (0, 3)}
DST_ROW = {1: 0, 0: 3, -1: 7}
SRC_COL = {1: (3, 3), 0: (0, 6), -1: (0, 3)}
DST_COL = {1: 0, 0: 3, -1: 9}


def remote(src, dst, send, recv, where):
    return pltpu.make_async_remote_copy(
        src_ref=src, dst_ref=dst, send_sem=send, recv_sem=recv, device_id=where, device_id_type=MESH
    )


def greet(where):
    barrier = pltpu.get_barrier_semaphore()
    for device in where:
        pl.semaphore_signal(barrier, inc=1, device_id=device, device_id_type=MESH)
    pl.semaphore_wait(barrier, len(where))


def halo_copies(pad, row, col, send, recv):
    out = []
    for k, (a, b) in enumerate(DIRS):
        r0, nr = SRC_ROW[a]
        c0, nc = SRC_COL[b]
        where = (lax.rem(row + a + N_ROW, N_ROW), lax.rem(col + b + N_COL, N_COL))
        out.append(
            remote(
                pad.at[pl.ds(3 + r0, nr), pl.ds(3 + c0, nc)],
                pad.at[pl.ds(DST_ROW[a], nr), pl.ds(DST_COL[b], nc)],
                send.at[k],
                recv.at[k],
                where,
            )
        )
    return out


def widen(pad, wide, row, col):
    top = jnp.where(row == 0, 0.0, 1.0)
    bottom = jnp.where(row == N_ROW - 1, 0.0, 1.0)
    left = jnp.where(col == 0, 0.0, 1.0)
    right = jnp.where(col == N_COL - 1, 0.0, 1.0)
    for a in range(ROWS + 6):
        edge = top if a < 3 else bottom if a >= 7 else 1.0
        wide[a, pl.ds(0, 3)] = pad[a, pl.ds(0, 3)].astype(F32) * (edge * left)
        if a < 3 or a >= 7:
            wide[a, pl.ds(3, 6)] = pad[a, pl.ds(3, 6)].astype(F32) * edge
        else:
            wide[a, pl.ds(3, 6)] = pad[a, pl.ds(3, 6)].astype(F32)
        wide[a, pl.ds(9, 3)] = pad[a, pl.ds(9, 3)].astype(F32) * (edge * right)


def row_of_taps(wide, kern, i, flip):
    def step(p, acc):
        line = wide[i + (6 - p if flip else p)]
        for q in range(7):
            s = 6 - q if flip else q
            acc = acc + line[s : s + COLS] * kern[p * 7 + q]
        return acc

    return lax.fori_loop(0, 7, step, jnp.zeros((COLS, SUB, LANE), F32))


def forward_kernel(
    feat, kern, gain, bias, slots, normed, slots_all, mixed, pad,
    wide, flat, halo_s, halo_r, n_s, n_r, g_s, g_r,
):
    row, col = lax.axis_index("row"), lax.axis_index("col")
    y, x = col // NX, lax.rem(col, NX)
    peer = lambda dy, dx: lax.rem(y + dy + NY, NY) * NX + lax.rem(x + dx + NX, NX)
    wherey = [(row, peer(dy, 0)) for dy in range(1, NY)]
    wherex = [(row, peer(0, dx)) for dx in range(1, NX)]
    around = [
        (lax.rem(row + a + N_ROW, N_ROW), lax.rem(col + b + N_COL, N_COL)) for a, b in DIRS
    ]
    pad[pl.ds(3, ROWS), pl.ds(3, COLS)] = feat[...]
    slots_all[col] = slots[...]
    greet(around + wherey + wherex)
    halo = halo_copies(pad, row, col, halo_s, halo_r)
    for c in halo:
        c.start()

    def own(ref, send, recv):
        for dy in range(1, NY):
            yield remote(ref.at[col], ref.at[col], send.at[dy, 0], recv.at[dy, 0], wherey[dy - 1])
        for dx in range(1, NX):
            yield remote(ref.at[col], ref.at[col], send.at[0, dx], recv.at[0, dx], wherex[dx - 1])

    def passed(ref, send, recv, dy, dx):
        block = ref.at[peer(-dy, 0)]
        return remote(block, block, send.at[dy, dx], recv.at[dy, dx], wherex[dx - 1])

    def came(ref, send, recv, dy, dx):
        block = ref.at[peer(-dy, -dx)]
        return remote(block, block, send.at[dy, dx], recv.at[dy, dx], (row, peer(dy, dx)))

    for c in own(slots_all, g_s, g_r):
        c.start()
    for c in halo:
        c.wait_recv()
    widen(pad, wide, row, col)

    def line(i, _):
        acc = row_of_taps(wide, kern, i, False)
        for j in range(COLS):
            flat[pl.ds(pl.multiple_of((i * COLS + j) * 16, 16), SUB)] = acc[j]
        return 0

    lax.fori_loop(0, ROWS, line, 0)
    for g in range(SUB):
        mixed[:, pl.ds(g * LANE, LANE)] = flat[pl.ds(g, PIX, stride=16)]
    m = mixed[...]
    centred = m - jnp.mean(m, axis=-1, keepdims=True)
    var = jnp.mean(centred * centred, axis=-1, keepdims=True)
    normed[col] = (centred * lax.rsqrt(var + 1e-06) * gain[...] + bias[...]).astype(BF16)
    for c in own(normed, n_s, n_r):
        c.start()
    for ref, send, recv in ((slots_all, g_s, g_r), (normed, n_s, n_r)):
        for dy in range(1, NY):
            came(ref, send, recv, dy, 0).wait_recv()
            for dx in range(1, NX):
                passed(ref, send, recv, dy, dx).start()
    for ref, send, recv in ((slots_all, g_s, g_r), (normed, n_s, n_r)):
        for dx in range(1, NX):
            for dy in range(NY):
                came(ref, send, recv, dy, dx).wait_recv()
    for ref, send, recv in ((slots_all, g_s, g_r), (normed, n_s, n_r)):
        for c in own(ref, send, recv):
            c.wait_send()
        for dy in range(1, NY):
            for dx in range(1, NX):
                passed(ref, send, recv, dy, dx).wait_send()
    for c in halo:
        c.wait_send()


def forward(feat, kern, gain, bias, slots):
    vm = pl.BlockSpec(memory_space=pltpu.VMEM)
    dma = pltpu.SemaphoreType.DMA
    return pl.pallas_call(
        forward_kernel,
        out_shape=(
            jax.ShapeDtypeStruct((N_COL, PIX, D), BF16),
            jax.ShapeDtypeStruct((N_COL, SLOT_PAD, D), BF16),
            jax.ShapeDtypeStruct((PIX, D), F32),
            jax.ShapeDtypeStruct((ROWS + 6, COLS + 6, SUB, LANE), BF16),
        ),
        in_specs=[vm] * 5,
        out_specs=[vm] * 4,
        scratch_shapes=[
            pltpu.VMEM((ROWS + 6, COLS + 6, SUB, LANE), F32),
            pltpu.VMEM((PIX * 16, LANE), F32),
            dma((8,)), dma((8,)),
            dma((NY, NX)), dma((NY, NX)),
            dma((NY, NX)), dma((NY, NX)),
        ],
        compiler_params=pltpu.CompilerParams(
            collective_id=0, has_side_effects=True, vmem_limit_bytes=VMEM_LIMIT
        ),
    )(feat, kern, gain, bias, slots)


def backward_kernel(
    ng, part, up, down, mixed, gain, kern, pad, og, slot, text,
    seq, gin, gker, gup, gdown,
    ng_in, part_in, up0, down0, up1, down1, up2, down2, up_h, down_h, up_c, down_c,
    mgpad, wide, mwide, flat, ker, ker_in, ker_z, ker_q, ker_out,
    ng_s, ng_r, part_s, part_r, halo_s, halo_r, c_s, c_r, z_s, z_r, h_s, h_r,
    a_s, a_r, b_s, b_r, k1_s, k1_r, k2_s, k2_r, k3_s, k3_r, k4_s, k4_r,
):
    row, col = lax.axis_index("row"), lax.axis_index("col")
    core = lax.rem(row, NC)
    z = lax.rem(row // NC, NZ)
    yh = row // (NC * NZ)
    at = lambda yy, zz, cc: ((yy * NZ + zz) * NC + cc, col)
    colp = [(row, lax.rem(col + k, N_COL)) for k in range(1, N_COL)]
    colb = [lax.rem(col + k, N_COL) for k in range(1, N_COL)]
    colf = [lax.rem(col - k + N_COL, N_COL) for k in range(1, N_COL)]
    zb = [lax.rem(z + k, NZ) for k in range(1, NZ)]
    zf = [lax.rem(z - k + NZ, NZ) for k in range(1, NZ)]
    zp = [at(yh, k, core) for k in zb]
    twin = at(yh, z, 1 - core)
    far = at(1 - yh, z, core)
    diag = at(1 - yh, z, 1 - core)
    around = [
        (lax.rem(row + a + N_ROW, N_ROW), lax.rem(col + b + N_COL, N_COL)) for a, b in DIRS
    ]
    greet(colp + around + zp + [twin, far, diag])

    ng_copies = [
        remote(ng.at[colb[k]], ng_in.at[k], ng_s.at[k], ng_r.at[k], colp[k])
        for k in range(N_COL - 1)
    ]
    for c in ng_copies:
        c.start()
    pair_copies = [
        remote(down.at[1 - core], down0, c_s.at[0], c_r.at[0], twin),
        remote(up.at[1 - core], up0, c_s.at[1], c_r.at[1], twin),
    ]
    for c in pair_copies:
        c.start()
    part_copies = [
        remote(part.at[colb[k]], part_in.at[k], part_s.at[k], part_r.at[k], colp[k])
        for k in range(N_COL - 1)
    ]
    for c in part_copies:
        c.start()

    for c in pair_copies:
        c.wait_recv()
    for k in range(NZ):
        down_h[k] = (down[core, k].astype(F32) + down0[k].astype(F32)).astype(BF16)
        up_h[k] = (up[core, k].astype(F32) + up0[k].astype(F32)).astype(BF16)
    z_copies = []
    for k in range(NZ - 1):
        z_copies.append(
            remote(down_h.at[zb[k]], down1.at[k], z_s.at[0, k], z_r.at[0, k], zp[k])
        )
        z_copies.append(remote(up_h.at[zb[k]], up1.at[k], z_s.at[1, k], z_r.at[1, k], zp[k]))
    for c in z_copies:
        c.start()

    for c in ng_copies:
        c.wait_recv()
    total = ng[col].astype(F32)
    for k in range(N_COL - 1):
        total = total + ng_in[k].astype(F32)
    m = mixed[...]
    centred = m - jnp.mean(m, axis=-1, keepdims=True)
    inv = lax.rsqrt(jnp.mean(centred * centred, axis=-1, keepdims=True) + 1e-06)
    hat = centred * inv
    dy = total * gain[...]
    dm = inv * (
        dy - jnp.mean(dy, axis=-1, keepdims=True) - hat * jnp.mean(dy * hat, axis=-1, keepdims=True)
    )
    dm = dm.astype(BF16).astype(F32)
    for g in range(SUB):
        flat[pl.ds(g, PIX, stride=16)] = dm[:, g * LANE : (g + 1) * LANE]
    for i in range(ROWS):
        for j in range(COLS):
            v = flat[pl.ds((i * COLS + j) * 16, SUB)]
            mgpad[3 + i, 3 + j] = v.astype(BF16)
            mwide[i, j] = v
    halo = halo_copies(mgpad, row, col, halo_s, halo_r)
    for c in halo:
        c.start()

    widen(pad, wide, row, col)

    def taps(p, _):
        acc = [jnp.zeros((SUB, LANE), F32) for _ in range(7)]
        for i in range(ROWS):
            line = wide[i + p]
            mine = mwide[i]
            for q in range(7):
                acc[q] = acc[q] + jnp.sum(line[q : q + COLS] * mine, axis=0)
        for q in range(7):
            t = p * 7 + q
            ker[t // 4, lax.rem(t, 4)] = acc[q].astype(BF16)
        return 0

    lax.fori_loop(0, 7, taps, 0)
    for t in range(49, 64):
        ker[t // 4, t % 4] = jnp.zeros((SUB, LANE), BF16)
    k1 = [
        remote(ker.at[colb[k]], ker_in.at[k], k1_s.at[k], k1_r.at[k], colp[k])
        for k in range(N_COL - 1)
    ]
    for c in k1:
        c.start()

    for c in z_copies:
        c.wait_recv()
    ds, us = down_h[z].astype(F32), up_h[z].astype(F32)
    for k in range(NZ - 1):
        ds = ds + down1[k].astype(F32)
        us = us + up1[k].astype(F32)
    down_c[...] = ds.astype(BF16)
    up_c[...] = us.astype(BF16)
    h_copies = [
        remote(down_c, down2, h_s.at[0], h_r.at[0], far),
        remote(up_c, up2, h_s.at[1], h_r.at[1], far),
    ]
    for c in h_copies:
        c.start()

    for c in k1:
        c.wait_recv()
    ks = ker[col].astype(F32)
    for k in range(N_COL - 1):
        ks = ks + ker_in[k].astype(F32)
    ker_z[z] = ks
    k2 = [
        remote(ker_z.at[z], ker_z.at[z], k2_s.at[k], k2_r.at[k], zp[k]) for k in range(NZ - 1)
    ]
    for c in k2:
        c.start()

    for c in halo:
        c.wait_recv()
    widen(mgpad, wide, row, col)

    def line(i, _):
        gin[i] = (row_of_taps(wide, kern, i, True) + og[i]).astype(BF16)
        return 0

    lax.fori_loop(0, ROWS, line, 0)

    for c in h_copies:
        c.wait_recv()
    gdown[core, z] = (down_c[...].astype(F32) + down2[...].astype(F32)).astype(BF16)
    gup[core, z] = (up_c[...].astype(F32) + up2[...].astype(F32)).astype(BF16)
    a_copies = []
    for k in range(NZ - 1):
        a_copies.append(
            remote(gdown.at[core, z], gdown.at[core, z], a_s.at[0, k], a_r.at[0, k], zp[k])
        )
        a_copies.append(remote(gup.at[core, z], gup.at[core, z], a_s.at[1, k], a_r.at[1, k], zp[k]))
    for c in a_copies:
        c.start()

    def across(ref, n, k, zz, cc):
        return remote(ref.at[cc, zz], ref.at[cc, zz], b_s.at[n, k], b_r.at[n, k], twin)

    across(gdown, 0, NZ - 1, z, core).start()
    across(gup, 1, NZ - 1, z, core).start()

    for c in k2:
        c.wait_recv()
    ks = ker_z[0]
    for k in range(1, NZ):
        ks = ks + ker_z[k]
    ker_q[yh * NC + core] = ks
    q = yh * NC + core
    k3 = [
        remote(ker_q.at[q], ker_q.at[q], k3_s.at[n], k3_r.at[n], where)
        for n, where in enumerate((twin, far, diag))
    ]
    for c in k3:
        c.start()

    for c in part_copies:
        c.wait_recv()
    tok = part[col].astype(F32)
    for k in range(N_COL - 1):
        tok = tok + part_in[k].astype(F32)
    seq[...] = jnp.where(slot[...] >= 0, tok.astype(BF16).astype(F32), text[...]).astype(BF16)

    for c in k3:
        c.wait_recv()
    ker_out[col] = (ker_q[0] + ker_q[1] + ker_q[2] + ker_q[3]).astype(BF16)
    k4 = [
        remote(ker_out.at[col], ker_out.at[col], k4_s.at[k], k4_r.at[k], colp[k])
        for k in range(N_COL - 1)
    ]
    for c in k4:
        c.start()
    for k in range(NZ - 1):
        for n, ref in enumerate((gdown, gup)):
            block = ref.at[core, zf[k]]
            remote(block, block, a_s.at[n, k], a_r.at[n, k], zp[k]).wait_recv()
            across(ref, n, k, zf[k], core).start()
    for k in range(N_COL - 1):
        block = ker_out.at[colf[k]]
        remote(block, block, k4_s.at[k], k4_r.at[k], colp[k]).wait_recv()
    for t in range(49):
        gker[t] = ker_out[t // 4, t % 4].astype(F32)
    for n, ref in enumerate((gdown, gup)):
        for k in range(NZ - 1):
            across(ref, n, k, zf[k], 1 - core).wait_recv()
        across(ref, n, NZ - 1, z, 1 - core).wait_recv()
        for k in range(NZ - 1):
            across(ref, n, k, zf[k], core).wait_send()
        across(ref, n, NZ - 1, z, core).wait_send()
    for c in ng_copies + pair_copies + part_copies + z_copies + halo + k1 + h_copies + k2:
        c.wait_send()
    for c in a_copies + k3 + k4:
        c.wait_send()


def backward(ng, part, up, down, mixed, gain, kern, pad, og, slot, text):
    vm = pl.BlockSpec(memory_space=pltpu.VMEM)
    dma = pltpu.SemaphoreType.DMA
    v = pltpu.VMEM
    w = D // NZ // NC
    h = HID // NZ // NC
    return pl.pallas_call(
        backward_kernel,
        out_shape=(
            jax.ShapeDtypeStruct((SLOT_PAD, D), BF16),
            jax.ShapeDtypeStruct((ROWS, COLS, SUB, LANE), BF16),
            jax.ShapeDtypeStruct((49, SUB, LANE), F32),
            jax.ShapeDtypeStruct((NC, NZ, w, HID), BF16),
            jax.ShapeDtypeStruct((NC, NZ, h, D), BF16),
        ),
        in_specs=[vm] * 11,
        out_specs=[vm] * 5,
        scratch_shapes=[
            v((N_COL - 1, PIX, D), BF16),
            v((N_COL - 1, SLOT_PAD, D), BF16),
            v((NZ, w, HID), BF16), v((NZ, h, D), BF16),
            v((NZ - 1, w, HID), BF16), v((NZ - 1, h, D), BF16),
            v((w, HID), BF16), v((h, D), BF16),
            v((NZ, w, HID), BF16), v((NZ, h, D), BF16),
            v((w, HID), BF16), v((h, D), BF16),
            v((ROWS + 6, COLS + 6, SUB, LANE), BF16),
            v((ROWS + 6, COLS + 6, SUB, LANE), F32),
            v((ROWS, COLS, SUB, LANE), F32),
            v((PIX * 16, LANE), F32),
            v((16, 4, SUB, LANE), BF16),
            v((N_COL - 1, 4, SUB, LANE), BF16),
            v((NZ, 4, SUB, LANE), F32),
            v((4, 4, SUB, LANE), F32),
            v((16, 4, SUB, LANE), BF16),
            dma((15,)), dma((15,)), dma((15,)), dma((15,)), dma((8,)), dma((8,)),
            dma((2,)), dma((2,)), dma((2, 7)), dma((2, 7)), dma((2,)), dma((2,)),
            dma((2, 7)), dma((2, 7)), dma((2, 8)), dma((2, 8)),
            dma((15,)), dma((15,)), dma((7,)), dma((7,)), dma((3,)), dma((3,)),
            dma((15,)), dma((15,)),
        ],
        compiler_params=pltpu.CompilerParams(
            collective_id=1, has_side_effects=True, vmem_limit_bytes=VMEM_LIMIT
        ),
    )(ng, part, up, down, mixed, gain, kern, pad, og, slot, text)


def gelu_tanh(value):
    return jax.nn.gelu(value, approximate=True)


def local(
    features, kernel, ln_gain, ln_bias, w_up, b_up, w_down, layer_scale,
    text_embed, slot_token, seq_grad,
):
    me = lax.axis_index("col")
    kern = kernel.reshape(49, SUB, LANE)
    feat = features.reshape(ROWS, COLS, SUB, LANE)
    gain, bias = ln_gain.reshape(1, D), ln_bias.reshape(1, D)
    tail = jnp.pad(slot_token.astype(BF16).reshape(1, SLOTS), ((0, 3), (0, D - SLOTS)))
    slots = jnp.concatenate([seq_grad, tail], axis=0)
    normed, slots_all, mixed, pad = forward(feat, kern, gain, bias, slots)

    band = normed.reshape(N_COL * PIX, D)
    held = slots_all[:, SLOTS, :SLOT_PAD].astype(jnp.int32)
    held = jnp.where(lax.broadcasted_iota(jnp.int32, held.shape, 1) < SLOTS, held, -1)
    pix = np.arange(PIX)
    inner = (pix // COLS // 2) * 3 + (pix % COLS) // 2
    token = (np.arange(N_COL)[:, None] * 6 + inner[None, :]).reshape(-1)
    select = (jnp.asarray(token, jnp.int32)[:, None] == held.reshape(-1)[None, :]).astype(BF16)
    mine = (
        (jnp.asarray(inner, jnp.int32)[:, None] + me * 6) == held.reshape(-1)[None, :]
    ).astype(BF16)
    every = slots_all.reshape(N_COL * SLOT_PAD, D)
    out_grad = jnp.dot(select, every, preferred_element_type=F32) * 0.25
    bg = (layer_scale * out_grad).astype(BF16)
    og = (jnp.dot(mine, every, preferred_element_type=F32) * 0.25).reshape(ROWS, COLS, SUB, LANE)
    pre = jnp.dot(band, w_up, preferred_element_type=F32) + b_up
    act = gelu_tanh(pre).astype(BF16)
    act_grad = jnp.einsum("pd,hd->ph", bg, w_down, preferred_element_type=F32)
    pre_grad = jax.vjp(gelu_tanh, pre)[1](act_grad)[0].astype(BF16)
    ng = jnp.einsum("ph,dh->pd", pre_grad, w_up, preferred_element_type=F32).astype(BF16)
    down = jnp.einsum("ph,pd->hd", act, bg, preferred_element_type=F32).astype(BF16)
    up = jnp.einsum("pd,ph->dh", band, pre_grad, preferred_element_type=F32).astype(BF16)
    pooled = (jnp.einsum("ps,ph->sh", select, act, preferred_element_type=F32) * 0.25).astype(BF16)
    part = layer_scale * jnp.dot(pooled, w_down, preferred_element_type=F32)
    part = part + 0.25 * jnp.einsum(
        "ps,pd->sd", mine, features.reshape(PIX, D), preferred_element_type=F32
    )
    part = part.astype(BF16)

    slot = jnp.pad(slot_token, (0, SLOT_PAD - SLOTS), constant_values=-1)[:, None]
    text = jnp.pad(text_embed.astype(F32), ((0, SLOT_PAD - SLOTS), (0, 0)))
    seq, gin, gker, gup, gdown = backward(
        ng.reshape(N_COL, PIX, D),
        part.reshape(N_COL, SLOT_PAD, D),
        up.reshape(NC, NZ, D // NC // NZ, HID),
        down.reshape(NC, NZ, HID // NC // NZ, D),
        mixed, gain, kern, pad, og,
        jnp.broadcast_to(slot, (SLOT_PAD, D)), text,
    )
    return (
        seq[:SLOTS],
        gin.reshape(ROWS, COLS, D),
        gker.reshape(49, D),
        gup.reshape(D, HID),
        gdown.reshape(HID, D),
    )


def solution(mesh):
    placed = (
        P("row", "col", None), P(), P(), P(), P(None, "col"), P("col"), P("col", None), P(),
        P(("row", "col"), None), P(("row", "col")), P(("row", "col"), None),
    )
    return jax.shard_map(
        local,
        mesh=mesh,
        in_specs=placed,
        out_specs=(
            P(("row", "col"), None), P("row", "col", None), P(), P(None, "col"), P("col", None),
        ),
        check_vma=False,
    )
```

```python
import jax
import jax.numpy as jnp
from jax import lax
from jax.experimental import pallas as pl
from jax.experimental.pallas import tpu as pltpu
from jax.sharding import PartitionSpec as P

F32, BF16 = jnp.float32, jnp.bfloat16
D, LANE, SUB = 1536, 128, 12
ROWS, COLS, PIX, SLOTS, SLOT_PAD = 4, 6, 24, 12, 16
N_ROW, N_COL = 32, 16
NX, NY = 4, 4
NZ, NC = 8, 2
HID = 256
DIRS = [(a, b) for a in (-1, 0, 1) for b in (-1, 0, 1) if (a, b) != (0, 0)]
MESH = pl.DeviceIdType.MESH
VMEM_LIMIT = 48 * 1024 * 1024
SRC_ROW = {1: (1, 3), 0: (0, 4), -1: (0, 3)}
DST_ROW = {1: 0, 0: 3, -1: 7}
SRC_COL = {1: (3, 3), 0: (0, 6), -1: (0, 3)}
DST_COL = {1: 0, 0: 3, -1: 9}


def remote(src, dst, send, recv, where):
    return pltpu.make_async_remote_copy(
        src_ref=src, dst_ref=dst, send_sem=send, recv_sem=recv, device_id=where, device_id_type=MESH
    )


def greet(where):
    barrier = pltpu.get_barrier_semaphore()
    for device in where:
        pl.semaphore_signal(barrier, inc=1, device_id=device, device_id_type=MESH)
    pl.semaphore_wait(barrier, len(where))


def halo_copies(pad, row, col, send, recv):
    out = []
    for k, (a, b) in enumerate(DIRS):
        r0, nr = SRC_ROW[a]
        c0, nc = SRC_COL[b]
        where = (lax.rem(row + a + N_ROW, N_ROW), lax.rem(col + b + N_COL, N_COL))
        out.append(
            remote(
                pad.at[pl.ds(3 + r0, nr), pl.ds(3 + c0, nc)],
                pad.at[pl.ds(DST_ROW[a], nr), pl.ds(DST_COL[b], nc)],
                send.at[k],
                recv.at[k],
                where,
            )
        )
    return out


def widen(pad, wide, row, col):
    top = jnp.where(row == 0, 0.0, 1.0)
    bottom = jnp.where(row == N_ROW - 1, 0.0, 1.0)
    left = jnp.where(col == 0, 0.0, 1.0)
    right = jnp.where(col == N_COL - 1, 0.0, 1.0)
    for a in range(ROWS + 6):
        edge = top if a < 3 else bottom if a >= 7 else 1.0
        wide[a, pl.ds(0, 3)] = pad[a, pl.ds(0, 3)].astype(F32) * (edge * left)
        if a < 3 or a >= 7:
            wide[a, pl.ds(3, 6)] = pad[a, pl.ds(3, 6)].astype(F32) * edge
        else:
            wide[a, pl.ds(3, 6)] = pad[a, pl.ds(3, 6)].astype(F32)
        wide[a, pl.ds(9, 3)] = pad[a, pl.ds(9, 3)].astype(F32) * (edge * right)


def row_of_taps(wide, kern, i, flip):
    def step(p, acc):
        line = wide[i + (6 - p if flip else p)]
        for q in range(7):
            s = 6 - q if flip else q
            tap = kern[pl.ds(pl.multiple_of((p * 7 + q) * 16, 16), SUB)]
            acc = acc + line[s : s + COLS] * tap
        return acc

    return lax.fori_loop(0, 7, step, jnp.zeros((COLS, SUB, LANE), F32))


def dot(a, b, ca, cb):
    return lax.dot_general(a, b, (((ca,), (cb,)), ((), ())), preferred_element_type=F32)


def whole_kernel(
    feat, kern, small, slots, w_up, w_down, text,
    seq, gin, gker, gup, gdown,
    pad, wide, flat, kflat, feat2, mixed, normed, band, every, select, bg, og, act_grad,
    act, pre_grad, ng, ng_x, ng_t, ng_y, part, part_x, part_t, part_y,
    up, down, up0, down0, up1, down1, up2, down2, up_h, down_h, up_c, down_c,
    mgpad, mwide, ker, ker_in, ker_z, ker_q, ker_out,
    f_s, f_r, n_s, n_r, g_s, g_r, nx_s, nx_r, ny_s, ny_r, px_s, px_r, py_s, py_r, halo_s, halo_r,
    c_s, c_r, z_s, z_r, h_s, h_r, a_s, a_r, b_s, b_r, k1_s, k1_r, k2_s, k2_r, k3_s, k3_r, k4_s, k4_r,
):
    row, col = lax.axis_index("row"), lax.axis_index("col")
    y, x = col // NX, lax.rem(col, NX)
    core = lax.rem(row, NC)
    z = lax.rem(row // NC, NZ)
    yh = row // (NC * NZ)
    at = lambda yy, zz, cc: ((yy * NZ + zz) * NC + cc, col)
    peer = lambda dy, dx: lax.rem(y + dy + NY, NY) * NX + lax.rem(x + dx + NX, NX)
    yp = [(row, peer(dy, 0)) for dy in range(1, NY)]
    xp = [(row, peer(0, dx)) for dx in range(1, NX)]
    colp = [(row, lax.rem(col + k, N_COL)) for k in range(1, N_COL)]
    colb = [lax.rem(col + k, N_COL) for k in range(1, N_COL)]
    colf = [lax.rem(col - k + N_COL, N_COL) for k in range(1, N_COL)]
    zb = [lax.rem(z + k, NZ) for k in range(1, NZ)]
    zf = [lax.rem(z - k + NZ, NZ) for k in range(1, NZ)]
    zp = [at(yh, k, core) for k in zb]
    twin = at(yh, z, 1 - core)
    far = at(1 - yh, z, core)
    diag = at(1 - yh, z, 1 - core)
    around = [
        (lax.rem(row + a + N_ROW, N_ROW), lax.rem(col + b + N_COL, N_COL)) for a, b in DIRS
    ]
    gain, bias, scale = small[0:1], small[1:2], small[2:3]
    slot_rows = lambda d: pl.ds(pl.multiple_of(d * SLOT_PAD, SLOT_PAD), SLOT_PAD)

    pad[pl.ds(3, ROWS), pl.ds(3, COLS)] = feat[...]
    every[slot_rows(col)] = slots[...]
    for g in range(SUB):
        kflat[pl.ds(g, 49, stride=16)] = kern[:, g * LANE : (g + 1) * LANE]
    for i in range(ROWS):
        for j in range(COLS):
            flat[pl.ds((i * COLS + j) * 16, SUB)] = feat[i, j].astype(F32)
    feat2[...] = jnp.zeros_like(feat2)
    for g in range(SUB):
        feat2[pl.ds(0, PIX), pl.ds(g * LANE, LANE)] = flat[pl.ds(g, PIX, stride=16)]
    greet(around + colp + zp + [twin, far, diag])

    f_halo = halo_copies(pad, row, col, f_s, f_r)
    for c in f_halo:
        c.start()

    n_at = lambda d: normed.at[d]
    g_at = lambda d: every.at[slot_rows(d)]

    def own(at_, send, recv):
        out = []
        for dy in range(1, NY):
            out.append(remote(at_(col), at_(col), send.at[dy, 0], recv.at[dy, 0], yp[dy - 1]))
        for dx in range(1, NX):
            out.append(remote(at_(col), at_(col), send.at[0, dx], recv.at[0, dx], xp[dx - 1]))
        return out

    def passed(at_, send, recv, dy, dx):
        b = peer(-dy, 0)
        return remote(at_(b), at_(b), send.at[dy, dx], recv.at[dy, dx], xp[dx - 1])

    def came(at_, send, recv, dy, dx):
        b = peer(-dy, -dx)
        return remote(at_(b), at_(b), send.at[dy, dx], recv.at[dy, dx], (row, peer(dy, dx)))

    g_all, n_all = (g_at, g_s, g_r), (n_at, n_s, n_r)

    def onward(ref):
        for dy in range(1, NY):
            came(*ref, dy, 0).wait_recv()
            for dx in range(1, NX):
                passed(*ref, dy, dx).start()

    def arrived(ref):
        for dx in range(1, NX):
            for dy in range(NY):
                came(*ref, dy, dx).wait_recv()

    for c in own(*g_all):
        c.start()
    for c in f_halo:
        c.wait_recv()
    onward(g_all)
    widen(pad, wide, row, col)

    def line(i, _):
        acc = row_of_taps(wide, kflat, i, False)
        for j in range(COLS):
            flat[pl.ds(pl.multiple_of((i * COLS + j) * 16, 16), SUB)] = acc[j]
        return 0

    lax.fori_loop(0, ROWS, line, 0)
    for g in range(SUB):
        mixed[:, pl.ds(g * LANE, LANE)] = flat[pl.ds(g, PIX, stride=16)]
    m = mixed[...]
    centred = m - jnp.mean(m, axis=-1, keepdims=True)
    var = jnp.mean(centred * centred, axis=-1, keepdims=True)
    normed[col] = (centred * lax.rsqrt(var + 1e-06) * gain + bias).astype(BF16)
    for c in own(*n_all):
        c.start()
    onward(n_all)

    arrived(g_all)
    names = jnp.zeros((SLOT_PAD, 256), F32)
    for d in range(N_COL):
        names = names + every[pl.ds(d * SLOT_PAD, SLOT_PAD), pl.ds(0, 256)].astype(F32)
    names = names[SLOTS : SLOTS + 1] - 1.0

    def token_of(count, first):
        p = lax.broadcasted_iota(jnp.int32, (count, 1), 0)
        d = jnp.where(p >= PIX, 1, 0)
        p = p - d * PIX
        one = lambda c: jnp.where(c, 1, 0)
        i = one(p >= 6) + one(p >= 12) + one(p >= 18)
        j = p - i * COLS
        t = 3 * one(i >= 2) + one(j >= 2) + one(j >= 4)
        return ((first + d) * 6 + t).astype(F32)

    for d in range(0, N_COL, 2):
        hit = token_of(2 * PIX, d) == names
        select[pl.ds(d * PIX, 2 * PIX)] = jnp.where(hit, 1.0, 0.0).astype(BF16)
    p32 = lax.broadcasted_iota(jnp.int32, (32, 1), 0)
    hit = jnp.where(p32 < PIX, token_of(32, col), -9.0) == names
    mine = jnp.where(hit, 1.0, 0.0).astype(BF16)

    def grads(c, _):
        cut = pl.ds(pl.multiple_of(c * 512, 512), 512)
        g = dot(select[...], every[:, cut], 1, 0) * 0.25
        bg[:, cut] = (g * small[2:3, cut]).astype(BF16)
        og[:, cut] = dot(mine, every[:, cut], 1, 0) * 0.25
        return 0

    lax.fori_loop(0, 3, grads, 0)

    def hidden_grads(r, _):
        cut = pl.ds(pl.multiple_of(r * 128, 128), 128)
        act_grad[cut] = dot(bg[cut], w_down[...], 1, 1)
        return 0

    lax.fori_loop(0, 3, hidden_grads, 0)

    arrived(n_all)
    for d in range(0, N_COL, 2):
        two = jnp.concatenate([normed[d].astype(F32), normed[d + 1].astype(F32)], axis=0)
        band[pl.ds(d * PIX, 2 * PIX)] = two.astype(BF16)

    def hidden(r, _):
        cut = pl.ds(pl.multiple_of(r * 128, 128), 128)
        v = dot(band[cut], w_up[...], 1, 0) + small[3:4, 0:HID]
        k0, k1 = 0.7978845608028654, 0.044715
        t = jnp.tanh(k0 * (v + k1 * v * v * v))
        act[cut] = (0.5 * v * (1.0 + t)).astype(BF16)
        slope = 0.5 * (1.0 + t) + 0.5 * v * (1.0 - t * t) * (k0 * (1.0 + 3.0 * k1 * v * v))
        pre_grad[cut] = (act_grad[cut] * slope).astype(BF16)
        return 0

    lax.fori_loop(0, 3, hidden, 0)

    def back(c, _):
        cut = pl.ds(pl.multiple_of(c * 512, 512), 512)
        v = dot(pre_grad[...], w_up[cut], 1, 1)
        for d in range(N_COL):
            ng[d, :, cut] = v[d * PIX : (d + 1) * PIX].astype(BF16)
        return 0

    lax.fori_loop(0, 3, back, 0)

    def across_x(at_, to, send, recv):
        out = {}
        for dy in (1, 2, 3, 0):
            for dx in range(1, NX):
                out[dy, dx] = remote(
                    at_(peer(dy, dx)), to.at[dx - 1, dy], send.at[dx, dy], recv.at[dx, dy],
                    xp[dx - 1],
                )
        return out

    def along_y(at_, xs, came_x, held, to, send, recv):
        out = []
        for dy in range(1, NY):
            v = at_(peer(dy, 0))[...].astype(F32)
            for dx in range(1, NX):
                xs[dy, dx].wait_recv()
                v = v + came_x[dx - 1, dy].astype(F32)
            held[dy - 1] = v.astype(BF16)
            out.append(
                remote(held.at[dy - 1], to.at[dy - 1], send.at[dy - 1], recv.at[dy - 1], yp[dy - 1])
            )
            out[-1].start()
        return out

    def at_home(at_, xs, came_x, ys, came_y):
        v = at_(col)[...].astype(F32)
        for dx in range(1, NX):
            xs[0, dx].wait_recv()
            v = v + came_x[dx - 1, 0].astype(F32)
        for dy in range(1, NY):
            ys[dy - 1].wait_recv()
            v = v + came_y[dy - 1].astype(F32)
        return v

    ng_at = lambda d: ng.at[d]
    ng_xs = across_x(ng_at, ng_x, nx_s, nx_r)
    for c in ng_xs.values():
        c.start()

    def down_part(c, _):
        cut = pl.ds(pl.multiple_of(c * 512, 512), 512)
        v = dot(act[...], bg[:, cut], 0, 0)
        for k in range(NC * NZ):
            down[k // NZ, k % NZ, :, cut] = v[k * 16 : (k + 1) * 16].astype(BF16)
        return 0

    lax.fori_loop(0, 3, down_part, 0)
    pair = [
        remote(down.at[1 - core], down0, c_s.at[0], c_r.at[0], twin),
        remote(up.at[1 - core], up0, c_s.at[1], c_r.at[1], twin),
    ]
    pair[0].start()
    for c in range(4):
        v = dot(band[:, c * 384 : (c + 1) * 384], pre_grad[...], 0, 0)
        for k in range(4):
            b = c * 4 + k
            up[b // NZ, b % NZ] = v[k * 96 : (k + 1) * 96].astype(BF16)
    pair[1].start()

    pooled = (dot(select[...], act[...], 0, 0) * 0.25).astype(BF16)

    def tokens(c, _):
        cut = pl.ds(pl.multiple_of(c * 512, 512), 512)
        v = dot(pooled, w_down[:, cut], 1, 0) * small[2:3, cut]
        v = v + 0.25 * dot(mine, feat2[:, cut].astype(BF16), 0, 0)
        part[:, cut] = v.astype(BF16)
        return 0

    lax.fori_loop(0, 3, tokens, 0)
    part_at = lambda d: part.at[slot_rows(d)]
    part_xs = across_x(part_at, part_x, px_s, px_r)
    for c in part_xs.values():
        c.start()

    for c in pair:
        c.wait_recv()
    for k in range(NZ):
        down_h[k] = (down[core, k].astype(F32) + down0[k].astype(F32)).astype(BF16)
        up_h[k] = (up[core, k].astype(F32) + up0[k].astype(F32)).astype(BF16)
    z_copies = []
    for k in range(NZ - 1):
        z_copies.append(
            remote(down_h.at[zb[k]], down1.at[k], z_s.at[0, k], z_r.at[0, k], zp[k])
        )
        z_copies.append(remote(up_h.at[zb[k]], up1.at[k], z_s.at[1, k], z_r.at[1, k], zp[k]))
    for c in z_copies:
        c.start()

    ng_ys = along_y(ng_at, ng_xs, ng_x, ng_t, ng_y, ny_s, ny_r)
    total = at_home(ng_at, ng_xs, ng_x, ng_ys, ng_y)
    m = mixed[...]
    centred = m - jnp.mean(m, axis=-1, keepdims=True)
    inv = lax.rsqrt(jnp.mean(centred * centred, axis=-1, keepdims=True) + 1e-06)
    hat = centred * inv
    dy_ = total * gain
    dm = inv * (
        dy_
        - jnp.mean(dy_, axis=-1, keepdims=True)
        - hat * jnp.mean(dy_ * hat, axis=-1, keepdims=True)
    )
    dm = dm.astype(BF16).astype(F32)
    for g in range(SUB):
        flat[pl.ds(g, PIX, stride=16)] = dm[:, g * LANE : (g + 1) * LANE]
    for i in range(ROWS):
        for j in range(COLS):
            v = flat[pl.ds((i * COLS + j) * 16, SUB)]
            mgpad[3 + i, 3 + j] = v.astype(BF16)
            mwide[i, j] = v
    halo = halo_copies(mgpad, row, col, halo_s, halo_r)
    for c in halo:
        c.start()

    def taps(p, _):
        acc = [jnp.zeros((SUB, LANE), F32) for _ in range(7)]
        for i in range(ROWS):
            line = wide[i + p]
            own_line = mwide[i]
            for q in range(7):
                acc[q] = acc[q] + jnp.sum(line[q : q + COLS] * own_line, axis=0)
        for q in range(7):
            t = p * 7 + q
            ker[t // 4, lax.rem(t, 4)] = acc[q].astype(BF16)
        return 0

    lax.fori_loop(0, 7, taps, 0)
    for t in range(49, 64):
        ker[t // 4, t % 4] = jnp.zeros((SUB, LANE), BF16)
    k1 = [
        remote(ker.at[colb[k]], ker_in.at[k], k1_s.at[k], k1_r.at[k], colp[k])
        for k in range(N_COL - 1)
    ]
    for c in k1:
        c.start()
    part_ys = along_y(part_at, part_xs, part_x, part_t, part_y, py_s, py_r)

    for c in z_copies:
        c.wait_recv()
    ds, us = down_h[z].astype(F32), up_h[z].astype(F32)
    for k in range(NZ - 1):
        ds = ds + down1[k].astype(F32)
        us = us + up1[k].astype(F32)
    down_c[...] = ds.astype(BF16)
    up_c[...] = us.astype(BF16)
    h_copies = [
        remote(down_c, down2, h_s.at[0], h_r.at[0], far),
        remote(up_c, up2, h_s.at[1], h_r.at[1], far),
    ]
    for c in h_copies:
        c.start()

    for c in k1:
        c.wait_recv()
    ks = ker[col].astype(F32)
    for k in range(N_COL - 1):
        ks = ks + ker_in[k].astype(F32)
    ker_z[z] = ks
    k2 = [
        remote(ker_z.at[z], ker_z.at[z], k2_s.at[k], k2_r.at[k], zp[k]) for k in range(NZ - 1)
    ]
    for c in k2:
        c.start()

    for c in h_copies:
        c.wait_recv()
    gdown[core, z] = (down_c[...].astype(F32) + down2[...].astype(F32)).astype(BF16)
    gup[core, z] = (up_c[...].astype(F32) + up2[...].astype(F32)).astype(BF16)
    a_copies = []
    for k in range(NZ - 1):
        a_copies.append(
            remote(gdown.at[core, z], gdown.at[core, z], a_s.at[0, k], a_r.at[0, k], zp[k])
        )
        a_copies.append(remote(gup.at[core, z], gup.at[core, z], a_s.at[1, k], a_r.at[1, k], zp[k]))
    for c in a_copies:
        c.start()

    def across(ref, n, k, zz, cc):
        return remote(ref.at[cc, zz], ref.at[cc, zz], b_s.at[n, k], b_r.at[n, k], twin)

    across(gdown, 0, NZ - 1, z, core).start()
    across(gup, 1, NZ - 1, z, core).start()

    for c in k2:
        c.wait_recv()
    ks = ker_z[0]
    for k in range(1, NZ):
        ks = ks + ker_z[k]
    q = yh * NC + core
    ker_q[q] = ks
    k3 = [
        remote(ker_q.at[q], ker_q.at[q], k3_s.at[n], k3_r.at[n], where)
        for n, where in enumerate((twin, far, diag))
    ]
    for c in k3:
        c.start()

    for c in halo:
        c.wait_recv()
    widen(mgpad, wide, row, col)
    for g in range(SUB):
        flat[pl.ds(g, PIX, stride=16)] = og[pl.ds(0, PIX), pl.ds(g * LANE, LANE)]

    def line_back(i, _):
        v = row_of_taps(wide, kflat, i, True)
        for j in range(COLS):
            first = flat[pl.ds(pl.multiple_of((i * COLS + j) * 16, 16), SUB)]
            gin[i, j] = (v[j] + first).astype(BF16)
        return 0

    lax.fori_loop(0, ROWS, line_back, 0)

    tok = at_home(part_at, part_xs, part_x, part_ys, part_y)
    lanes = lax.broadcasted_iota(jnp.int32, (SLOT_PAD, 256), 1)
    rows = lax.broadcasted_iota(jnp.int32, (SLOT_PAD, 256), 0)
    named = slots[pl.ds(0, SLOT_PAD), pl.ds(0, 256)].astype(F32)[SLOTS : SLOTS + 1]
    live = jnp.sum(jnp.where(lanes == rows + col * SLOT_PAD, named, 0.0), axis=1, keepdims=True)
    seq[...] = jnp.where(
        live[:SLOTS] > 0.5, tok[:SLOTS].astype(BF16).astype(F32), text[...].astype(F32)
    ).astype(BF16)

    for c in k3:
        c.wait_recv()
    ker_out[col] = (ker_q[0] + ker_q[1] + ker_q[2] + ker_q[3]).astype(BF16)
    k4 = [
        remote(ker_out.at[col], ker_out.at[col], k4_s.at[k], k4_r.at[k], colp[k])
        for k in range(N_COL - 1)
    ]
    for c in k4:
        c.start()
    for k in range(NZ - 1):
        for n, ref in enumerate((gdown, gup)):
            block = ref.at[core, zf[k]]
            remote(block, block, a_s.at[n, k], a_r.at[n, k], zp[k]).wait_recv()
            across(ref, n, k, zf[k], core).start()
    for k in range(N_COL - 1):
        block = ker_out.at[colf[k]]
        remote(block, block, k4_s.at[k], k4_r.at[k], colp[k]).wait_recv()
    for t in range(49):
        kflat[pl.ds(t * 16, SUB)] = ker_out[t // 4, t % 4].astype(F32)
    for g in range(SUB):
        gker[:, g * LANE : (g + 1) * LANE] = kflat[pl.ds(g, 49, stride=16)]
    for n, ref in enumerate((gdown, gup)):
        for k in range(NZ - 1):
            across(ref, n, k, zf[k], 1 - core).wait_recv()
        across(ref, n, NZ - 1, z, 1 - core).wait_recv()
        for k in range(NZ - 1):
            across(ref, n, k, zf[k], core).wait_send()
        across(ref, n, NZ - 1, z, core).wait_send()
    for ref in (g_all, n_all):
        for c in own(*ref):
            c.wait_send()
        for dy in range(1, NY):
            for dx in range(1, NX):
                passed(*ref, dy, dx).wait_send()
    for c in f_halo + list(ng_xs.values()) + list(part_xs.values()) + ng_ys + part_ys + pair:
        c.wait_send()
    for c in z_copies + halo + k1 + h_copies + k2 + a_copies + k3 + k4:
        c.wait_send()


def whole(feat, kern, small, slots, w_up, w_down, text):
    vm = pl.BlockSpec(memory_space=pltpu.VMEM)
    dma = pltpu.SemaphoreType.DMA
    v = pltpu.VMEM
    w = D // NZ // NC
    h = HID // NZ // NC
    band = N_COL * PIX
    every = N_COL * SLOT_PAD
    map_ = (ROWS + 6, COLS + 6, SUB, LANE)
    return pl.pallas_call(
        whole_kernel,
        out_shape=(
            jax.ShapeDtypeStruct((SLOTS, D), BF16),
            jax.ShapeDtypeStruct((ROWS, COLS, SUB, LANE), BF16),
            jax.ShapeDtypeStruct((49, D), F32),
            jax.ShapeDtypeStruct((NC, NZ, w, HID), BF16),
            jax.ShapeDtypeStruct((NC, NZ, h, D), BF16),
        ),
        in_specs=[vm] * 7,
        out_specs=[vm] * 5,
        scratch_shapes=[
            v(map_, BF16), v(map_, F32), v((PIX * 16, LANE), F32), v((49 * 16, LANE), F32),
            v((32, D), F32), v((PIX, D), F32),
            v((N_COL, PIX, D), BF16), v((band, D), BF16), v((every, D), BF16),
            v((band, every), BF16), v((band, D), BF16), v((32, D), F32),
            v((band, HID), F32), v((band, HID), BF16), v((band, HID), BF16),
            v((N_COL, PIX, D), BF16), v((NX - 1, NY, PIX, D), BF16),
            v((NY - 1, PIX, D), BF16), v((NY - 1, PIX, D), BF16),
            v((every, D), BF16), v((NX - 1, NY, SLOT_PAD, D), BF16),
            v((NY - 1, SLOT_PAD, D), BF16), v((NY - 1, SLOT_PAD, D), BF16),
            v((NC, NZ, w, HID), BF16), v((NC, NZ, h, D), BF16),
            v((NZ, w, HID), BF16), v((NZ, h, D), BF16),
            v((NZ - 1, w, HID), BF16), v((NZ - 1, h, D), BF16),
            v((w, HID), BF16), v((h, D), BF16),
            v((NZ, w, HID), BF16), v((NZ, h, D), BF16),
            v((w, HID), BF16), v((h, D), BF16),
            v(map_, BF16), v((ROWS, COLS, SUB, LANE), F32),
            v((16, 4, SUB, LANE), BF16), v((N_COL - 1, 4, SUB, LANE), BF16),
            v((NZ, 4, SUB, LANE), F32), v((4, 4, SUB, LANE), F32), v((16, 4, SUB, LANE), BF16),
            dma((8,)), dma((8,)), dma((NY, NX)), dma((NY, NX)), dma((NY, NX)), dma((NY, NX)),
            dma((NX, NY)), dma((NX, NY)), dma((3,)), dma((3,)),
            dma((NX, NY)), dma((NX, NY)), dma((3,)), dma((3,)),
            dma((8,)), dma((8,)),
            dma((2,)), dma((2,)), dma((2, 7)), dma((2, 7)), dma((2,)), dma((2,)),
            dma((2, 7)), dma((2, 7)), dma((2, 8)), dma((2, 8)),
            dma((15,)), dma((15,)), dma((7,)), dma((7,)), dma((3,)), dma((3,)),
            dma((15,)), dma((15,)),
        ],
        compiler_params=pltpu.CompilerParams(
            collective_id=0, has_side_effects=True, vmem_limit_bytes=VMEM_LIMIT
        ),
    )(feat, kern, small, slots, w_up, w_down, text)


def local(
    features, kernel, ln_gain, ln_bias, w_up, b_up, w_down, layer_scale,
    text_embed, slot_token, seq_grad,
):
    me = lax.axis_index("col")
    feat = features.reshape(ROWS, COLS, SUB, LANE)
    small = jnp.stack([ln_gain, ln_bias, layer_scale, jnp.pad(b_up, (0, D - HID))])
    name = jnp.tile(jnp.pad(slot_token + 1, (0, SLOT_PAD - SLOTS)), N_COL)
    name = jnp.where(lax.iota(jnp.int32, N_COL * SLOT_PAD) // SLOT_PAD == me, name, 0)
    tail = jnp.pad(name.astype(BF16)[None, :], ((0, 3), (0, D - N_COL * SLOT_PAD)))
    slots = jnp.concatenate([seq_grad, tail], axis=0)
    seq, gin, gker, gup, gdown = whole(feat, kernel, small, slots, w_up, w_down, text_embed)
    return (
        seq, gin.reshape(ROWS, COLS, D), gker, gup.reshape(D, HID), gdown.reshape(HID, D),
    )


def solution(mesh):
    placed = (
        P("row", "col", None), P(), P(), P(), P(None, "col"), P("col"), P("col", None), P(),
        P(("row", "col"), None), P(("row", "col")), P(("row", "col"), None),
    )
    return jax.shard_map(
        local,
        mesh=mesh,
        in_specs=placed,
        out_specs=(
            P(("row", "col"), None), P("row", "col", None), P(), P(None, "col"), P("col", None),
        ),
        check_vma=False,
    )
```

```python
import jax
import jax.numpy as jnp
from jax import lax
from jax.experimental import pallas as pl
from jax.experimental.pallas import tpu as pltpu
from jax.sharding import PartitionSpec as P

F32, BF16 = jnp.float32, jnp.bfloat16
D, LANE, SUB = 1536, 128, 12
ROWS, COLS, PIX, SLOTS, SLOT_PAD = 4, 6, 24, 12, 16
N_ROW, N_COL = 32, 16
NX, NY = 4, 4
NZ, NC = 8, 2
HID = 256
DIRS = [(a, b) for a in (-1, 0, 1) for b in (-1, 0, 1) if (a, b) != (0, 0)]
MESH = pl.DeviceIdType.MESH
VMEM_LIMIT = 48 * 1024 * 1024
SRC_ROW = {1: (1, 3), 0: (0, 4), -1: (0, 3)}
DST_ROW = {1: 0, 0: 3, -1: 7}
SRC_COL = {1: (3, 3), 0: (0, 6), -1: (0, 3)}
DST_COL = {1: 0, 0: 3, -1: 9}


def remote(src, dst, send, recv, where):
    return pltpu.make_async_remote_copy(
        src_ref=src, dst_ref=dst, send_sem=send, recv_sem=recv, device_id=where, device_id_type=MESH
    )


def greet(where):
    barrier = pltpu.get_barrier_semaphore()
    for device in where:
        pl.semaphore_signal(barrier, inc=1, device_id=device, device_id_type=MESH)
    return barrier


def halo_copies(pad, row, col, send, recv):
    out = []
    for k, (a, b) in enumerate(DIRS):
        r0, nr = SRC_ROW[a]
        c0, nc = SRC_COL[b]
        where = (lax.rem(row + a + N_ROW, N_ROW), lax.rem(col + b + N_COL, N_COL))
        out.append(
            remote(
                pad.at[pl.ds(3 + r0, nr), pl.ds(3 + c0, nc)],
                pad.at[pl.ds(DST_ROW[a], nr), pl.ds(DST_COL[b], nc)],
                send.at[k],
                recv.at[k],
                where,
            )
        )
    return out


def widen(pad, wide, row, col):
    top = jnp.where(row == 0, 0.0, 1.0)
    bottom = jnp.where(row == N_ROW - 1, 0.0, 1.0)
    left = jnp.where(col == 0, 0.0, 1.0)
    right = jnp.where(col == N_COL - 1, 0.0, 1.0)
    for a in range(ROWS + 6):
        edge = top if a < 3 else bottom if a >= 7 else 1.0
        wide[a, pl.ds(0, 3)] = pad[a, pl.ds(0, 3)].astype(F32) * (edge * left)
        if a < 3 or a >= 7:
            wide[a, pl.ds(3, 6)] = pad[a, pl.ds(3, 6)].astype(F32) * edge
        else:
            wide[a, pl.ds(3, 6)] = pad[a, pl.ds(3, 6)].astype(F32)
        wide[a, pl.ds(9, 3)] = pad[a, pl.ds(9, 3)].astype(F32) * (edge * right)


def row_of_taps(wide, kern, i, flip):
    def step(p, acc):
        line = wide[i + (6 - p if flip else p)]
        for q in range(7):
            s = 6 - q if flip else q
            tap = kern[pl.ds(pl.multiple_of((p * 7 + q) * 16, 16), SUB)]
            acc = acc + line[s : s + COLS] * tap
        return acc

    return lax.fori_loop(0, 7, step, jnp.zeros((COLS, SUB, LANE), F32))


def dot(a, b, ca, cb):
    return lax.dot_general(a, b, (((ca,), (cb,)), ((), ())), preferred_element_type=F32)


def whole_kernel(
    feat, kern, ln_gain, ln_bias, b_up, layer_scale, slot, seq_grad, w_up_hbm, w_down_hbm, text_hbm,
    seq, gin, gker, gup, gdown,
    w_up, w_down, text, block,
    pad, wide, flat, kflat, feat2, mixed, normed, band, every, select, bg, og, act_grad,
    act, pre_grad, ng, ng_x, ng_t, ng_y, part, part_x, part_t, part_y,
    up, down, up0, down0, up1, down1, up2, down2, up_h, down_h, up_q, down_c,
    mgpad, mwide, ker, ker_p, ker_h, ker_in, ker_z, ker_z_in, ker_out,
    w_s, f_s, f_r, n_s, n_r, g_s, g_r,
    nx_s, nx_r, ny_s, ny_r, px_s, px_r, py_s, py_r, halo_s, halo_r,
    c_s, c_r, dz_s, dz_r, uz_s, uz_r, h_s, h_r,
    da_s, da_r, ua_s, ua_r, uf_s, uf_r, dt_s, dt_r, ut_s, ut_r,
    k0_s, k0_r, k1_s, k1_r, k2_s, k2_r, k4_s, k4_r, k5_s, k5_r,
):
    row, col = lax.axis_index("row"), lax.axis_index("col")
    y, x = col // NX, lax.rem(col, NX)
    core = lax.rem(row, NC)
    z = lax.rem(row // NC, NZ)
    yh = row // (NC * NZ)
    at = lambda yy, zz, cc: ((yy * NZ + zz) * NC + cc, col)
    peer = lambda dy, dx: lax.rem(y + dy + NY, NY) * NX + lax.rem(x + dx + NX, NX)
    yp = [(row, peer(dy, 0)) for dy in range(1, NY)]
    xp = [(row, peer(0, dx)) for dx in range(1, NX)]
    colp = [(row, lax.rem(col + k, N_COL)) for k in range(1, N_COL)]
    colb = [lax.rem(col + k, N_COL) for k in range(1, N_COL)]
    colf = [lax.rem(col - k + N_COL, N_COL) for k in range(1, N_COL)]
    zb = [lax.rem(z + k, NZ) for k in range(1, NZ)]
    zf = [lax.rem(z - k + NZ, NZ) for k in range(1, NZ)]
    zp = [at(yh, k, core) for k in zb]
    twin = at(yh, z, 1 - core)
    far = at(1 - yh, z, core)
    rowp = zp + [at(1 - yh, lax.rem(z + k, NZ), core) for k in range(NZ)]
    around = [
        (lax.rem(row + a + N_ROW, N_ROW), lax.rem(col + b + N_COL, N_COL)) for a, b in DIRS
    ]
    fetch = [
        pltpu.make_async_copy(a, b, w_s.at[k])
        for k, (a, b) in enumerate(((w_up_hbm, w_up), (w_down_hbm, w_down), (text_hbm, text)))
    ]
    for c in fetch:
        c.start()
    gain, bias = ln_gain[...].reshape(1, D), ln_bias[...].reshape(1, D)
    b_row = b_up[...].reshape(1, HID)
    slot_rows = lambda d: pl.ds(pl.multiple_of(d * SLOT_PAD, SLOT_PAD), SLOT_PAD)

    partners = around + colp + rowp + [twin]
    barrier = greet(partners)
    pad[pl.ds(3, ROWS), pl.ds(3, COLS)] = feat[...]
    lane = lax.broadcasted_iota(jnp.int32, (1, 256), 1)
    name = jnp.zeros((1, 256), jnp.int32)
    for r in range(SLOTS):
        name = jnp.where(lane == col * SLOT_PAD + r, slot[r] + 1, name)
    block[...] = jnp.zeros_like(block)
    block[pl.ds(0, SLOTS)] = seq_grad[...].astype(F32)
    block[pl.ds(SLOTS, 1), pl.ds(0, 256)] = name.astype(F32)
    every[slot_rows(col)] = block[...].astype(BF16)
    pl.semaphore_wait(barrier, len(partners))

    f_halo = halo_copies(pad, row, col, f_s, f_r)
    for c in f_halo:
        c.start()

    n_at = lambda d: normed.at[d]
    g_at = lambda d: every.at[slot_rows(d)]

    def own(at_, send, recv):
        out = []
        for dy in range(1, NY):
            out.append(remote(at_(col), at_(col), send.at[dy, 0], recv.at[dy, 0], yp[dy - 1]))
        for dx in range(1, NX):
            out.append(remote(at_(col), at_(col), send.at[0, dx], recv.at[0, dx], xp[dx - 1]))
        return out

    def passed(at_, send, recv, dy, dx):
        b = peer(-dy, 0)
        return remote(at_(b), at_(b), send.at[dy, dx], recv.at[dy, dx], xp[dx - 1])

    def came(at_, send, recv, dy, dx):
        b = peer(-dy, -dx)
        return remote(at_(b), at_(b), send.at[dy, dx], recv.at[dy, dx], (row, peer(dy, dx)))

    g_all, n_all = (g_at, g_s, g_r), (n_at, n_s, n_r)

    def onward(ref):
        for a in range(1, 4):
            came(*ref, a, 0).wait_recv()
            for b in range(1, 4):
                passed(*ref, a, b).start()

    def arrived(ref):
        for a in range(4):
            for b in range(1, 4):
                came(*ref, a, b).wait_recv()

    for c in own(*g_all):
        c.start()
    for g in range(SUB):
        kflat[pl.ds(g, 49, stride=16)] = kern[:, g * LANE : (g + 1) * LANE]
    for i in range(ROWS):
        for j in range(COLS):
            flat[pl.ds((i * COLS + j) * 16, SUB)] = feat[i, j].astype(F32)
    feat2[...] = jnp.zeros_like(feat2)
    for g in range(SUB):
        feat2[pl.ds(0, PIX), pl.ds(g * LANE, LANE)] = flat[pl.ds(g, PIX, stride=16)]
    for c in f_halo:
        c.wait_recv()
    onward(g_all)
    widen(pad, wide, row, col)

    def line(i, _):
        acc = row_of_taps(wide, kflat, i, False)
        for j in range(COLS):
            flat[pl.ds(pl.multiple_of((i * COLS + j) * 16, 16), SUB)] = acc[j]
        return 0

    lax.fori_loop(0, ROWS, line, 0)
    for g in range(SUB):
        mixed[:, pl.ds(g * LANE, LANE)] = flat[pl.ds(g, PIX, stride=16)]
    m = mixed[...]
    centred = m - jnp.mean(m, axis=-1, keepdims=True)
    var = jnp.mean(centred * centred, axis=-1, keepdims=True)
    normed[col] = (centred * lax.rsqrt(var + 1e-06) * gain + bias).astype(BF16)
    for c in own(*n_all):
        c.start()
    onward(n_all)

    arrived(g_all)
    slots_row = name.astype(F32)
    names = jnp.zeros((SLOT_PAD, 256), F32)
    for d in range(N_COL):
        names = names + every[pl.ds(d * SLOT_PAD, SLOT_PAD), pl.ds(0, 256)].astype(F32)
    names = names[SLOTS : SLOTS + 1] - 1.0

    def token_of(count, first):
        p = lax.broadcasted_iota(jnp.int32, (count, 1), 0)
        d = jnp.where(p >= PIX, 1, 0)
        p = p - d * PIX
        one = lambda c: jnp.where(c, 1, 0)
        i = one(p >= 6) + one(p >= 12) + one(p >= 18)
        j = p - i * COLS
        t = 3 * one(i >= 2) + one(j >= 2) + one(j >= 4)
        return ((first + d) * 6 + t).astype(F32)

    for d in range(0, N_COL, 2):
        hit = token_of(2 * PIX, d) == names
        select[pl.ds(d * PIX, 2 * PIX)] = jnp.where(hit, 1.0, 0.0).astype(BF16)
    p32 = lax.broadcasted_iota(jnp.int32, (32, 1), 0)
    hit = jnp.where(p32 < PIX, token_of(32, col), -9.0) == names
    mine = jnp.where(hit, 1.0, 0.0).astype(BF16)

    def grads(c, _):
        cut = pl.ds(pl.multiple_of(c * 512, 512), 512)
        g = dot(select[...], every[:, cut], 1, 0) * 0.25
        bg[:, cut] = (g * layer_scale[cut].reshape(1, 512)).astype(BF16)
        og[:, cut] = dot(mine, every[:, cut], 1, 0) * 0.25
        return 0

    for c in fetch:
        c.wait()
    lax.fori_loop(0, 3, grads, 0)

    def hidden_grads(r, _):
        cut = pl.ds(pl.multiple_of(r * 128, 128), 128)
        act_grad[cut] = dot(bg[cut], w_down[...], 1, 1)
        return 0

    lax.fori_loop(0, 3, hidden_grads, 0)

    arrived(n_all)
    for d in range(0, N_COL, 2):
        two = jnp.concatenate([normed[d].astype(F32), normed[d + 1].astype(F32)], axis=0)
        band[pl.ds(d * PIX, 2 * PIX)] = two.astype(BF16)

    def hidden(r, _):
        cut = pl.ds(pl.multiple_of(r * 128, 128), 128)
        v = dot(band[cut], w_up[...], 1, 0) + b_row
        k0, k1 = 0.7978845608028654, 0.044715
        t = jnp.tanh(k0 * (v + k1 * v * v * v))
        act[cut] = (0.5 * v * (1.0 + t)).astype(BF16)
        slope = 0.5 * (1.0 + t) + 0.5 * v * (1.0 - t * t) * (k0 * (1.0 + 3.0 * k1 * v * v))
        pre_grad[cut] = (act_grad[cut] * slope).astype(BF16)
        return 0

    lax.fori_loop(0, 3, hidden, 0)

    def back(c, _):
        cut = pl.ds(pl.multiple_of(c * 512, 512), 512)
        v = dot(pre_grad[...], w_up[cut], 1, 1)
        for d in range(N_COL):
            ng[d, :, cut] = v[d * PIX : (d + 1) * PIX].astype(BF16)
        return 0

    lax.fori_loop(0, 3, back, 0)

    def across_x(at_, to, send, recv):
        out = {}
        for dy in (1, 2, 3, 0):
            for dx in range(1, NX):
                out[dy, dx] = remote(
                    at_(peer(dy, dx)), to.at[dx - 1, dy], send.at[dx, dy], recv.at[dx, dy],
                    xp[dx - 1],
                )
        return out

    def along_y(at_, xs, came_x, held, to, send, recv):
        out = []
        for dy in range(1, NY):
            v = at_(peer(dy, 0))[...].astype(F32)
            for dx in range(1, NX):
                xs[dy, dx].wait_recv()
                v = v + came_x[dx - 1, dy].astype(F32)
            held[dy - 1] = v.astype(BF16)
            out.append(
                remote(held.at[dy - 1], to.at[dy - 1], send.at[dy - 1], recv.at[dy - 1], yp[dy - 1])
            )
            out[-1].start()
        return out

    def at_home(at_, xs, came_x, ys, came_y):
        v = at_(col)[...].astype(F32)
        for dx in range(1, NX):
            xs[0, dx].wait_recv()
            v = v + came_x[dx - 1, 0].astype(F32)
        for dy in range(1, NY):
            ys[dy - 1].wait_recv()
            v = v + came_y[dy - 1].astype(F32)
        return v

    ng_at = lambda d: ng.at[d]
    ng_xs = across_x(ng_at, ng_x, nx_s, nx_r)
    for c in ng_xs.values():
        c.start()

    def down_part(c, _):
        cut = pl.ds(pl.multiple_of(c * 512, 512), 512)
        v = dot(act[...], bg[:, cut], 0, 0)
        for k in range(NC * NZ):
            down[k // NZ, k % NZ, :, cut] = v[k * 16 : (k + 1) * 16].astype(BF16)
        return 0

    lax.fori_loop(0, 3, down_part, 0)
    pair = [
        remote(down.at[1 - core], down0, c_s.at[0], c_r.at[0], twin),
        remote(up.at[1 - core], up0, c_s.at[1], c_r.at[1], twin),
    ]
    pair[0].start()
    for c in range(4):
        v = dot(band[:, c * 384 : (c + 1) * 384], pre_grad[...], 0, 0)
        for k in range(8):
            up[c // 2, c % 2, k] = v[k * 48 : (k + 1) * 48].astype(BF16)
    pair[1].start()

    pooled = (dot(select[...], act[...], 0, 0) * 0.25).astype(BF16)

    def tokens(c, _):
        cut = pl.ds(pl.multiple_of(c * 512, 512), 512)
        v = dot(pooled, w_down[:, cut], 1, 0) * layer_scale[cut].reshape(1, 512)
        v = v + 0.25 * dot(mine, feat2[:, cut].astype(BF16), 0, 0)
        part[:, cut] = v.astype(BF16)
        return 0

    lax.fori_loop(0, 3, tokens, 0)
    part_at = lambda d: part.at[slot_rows(d)]
    part_xs = across_x(part_at, part_x, px_s, px_r)
    for c in part_xs.values():
        c.start()

    for c in pair:
        c.wait_recv()
    for k in range(NZ):
        down_h[k] = (down[core, k].astype(F32) + down0[k].astype(F32)).astype(BF16)
        for n in range(2):
            up_h[n, k] = (up[core, n, k].astype(F32) + up0[n, k].astype(F32)).astype(BF16)
    up_far = remote(up_h.at[1 - yh], up1, h_s.at[0], h_r.at[0], far)
    up_far.start()
    down_z = [
        remote(down_h.at[zb[k]], down1.at[k], dz_s.at[k], dz_r.at[k], zp[k]) for k in range(NZ - 1)
    ]
    for c in down_z:
        c.start()

    ng_ys = along_y(ng_at, ng_xs, ng_x, ng_t, ng_y, ny_s, ny_r)
    total = at_home(ng_at, ng_xs, ng_x, ng_ys, ng_y)
    m = mixed[...]
    centred = m - jnp.mean(m, axis=-1, keepdims=True)
    inv = lax.rsqrt(jnp.mean(centred * centred, axis=-1, keepdims=True) + 1e-06)
    hat = centred * inv
    dy_ = total * gain
    dm = inv * (
        dy_
        - jnp.mean(dy_, axis=-1, keepdims=True)
        - hat * jnp.mean(dy_ * hat, axis=-1, keepdims=True)
    )
    dm = dm.astype(BF16).astype(F32)
    for g in range(SUB):
        flat[pl.ds(g, PIX, stride=16)] = dm[:, g * LANE : (g + 1) * LANE]
    for i in range(ROWS):
        for j in range(COLS):
            v = flat[pl.ds((i * COLS + j) * 16, SUB)]
            mgpad[3 + i, 3 + j] = v.astype(BF16)
            mwide[i, j] = v
    halo = halo_copies(mgpad, row, col, halo_s, halo_r)
    for c in halo:
        c.start()

    def taps(p, _):
        acc = [jnp.zeros((SUB, LANE), F32) for _ in range(7)]
        for i in range(ROWS):
            line = wide[i + p]
            own_line = mwide[i]
            for q in range(7):
                acc[q] = acc[q] + jnp.sum(line[q : q + COLS] * own_line, axis=0)
        for q in range(7):
            t = p * 7 + q
            ker[lax.rem(t, 2), t // 4, lax.rem(t // 2, 2)] = acc[q].astype(BF16)
        return 0

    lax.fori_loop(0, 7, taps, 0)
    for t in range(49, 64):
        ker[t % 2, t // 4, t // 2 % 2] = jnp.zeros((SUB, LANE), BF16)
    k0 = remote(ker.at[1 - core], ker_p, k0_s.at[0], k0_r.at[0], twin)
    k0.start()

    k0.wait_recv()
    for k in range(16):
        ker_h[k] = (ker[core, k].astype(F32) + ker_p[k].astype(F32)).astype(BF16)
    k1 = [
        remote(ker_h.at[colb[k]], ker_in.at[k], k1_s.at[k], k1_r.at[k], colp[k])
        for k in range(N_COL - 1)
    ]
    for c in k1:
        c.start()
    for c in down_z:
        c.wait_recv()
    v = down_h[z].astype(F32)
    for k in range(NZ - 1):
        v = v + down1[k].astype(F32)
    down_c[...] = v.astype(BF16)
    down_far = remote(down_c, down2, h_s.at[1], h_r.at[1], far)
    down_far.start()
    up_far.wait_recv()
    for k in range(NZ):
        up_q[k] = (up_h[yh, k].astype(F32) + up1[k].astype(F32)).astype(BF16)
    up_z = [
        remote(up_q.at[zb[k]], up2.at[k], uz_s.at[k], uz_r.at[k], zp[k]) for k in range(NZ - 1)
    ]
    for c in up_z:
        c.start()

    part_ys = along_y(part_at, part_xs, part_x, part_t, part_y, py_s, py_r)

    for c in k1:
        c.wait_recv()
    v = ker_h[col].astype(F32)
    for k in range(N_COL - 1):
        v = v + ker_in[k].astype(F32)
    ker_z[...] = v.astype(BF16)
    place = yh * NZ + z
    ker_z_in[place] = ker_z[...]
    k2 = [
        remote(ker_z, ker_z_in.at[place], k2_s.at[k], k2_r.at[k], rowp[k]) for k in range(15)
    ]
    for c in k2:
        c.start()

    for c in halo:
        c.wait_recv()
    widen(mgpad, wide, row, col)
    for g in range(SUB):
        flat[pl.ds(g, PIX, stride=16)] = og[pl.ds(0, PIX), pl.ds(g * LANE, LANE)]

    def line_back(i, _):
        v = row_of_taps(wide, kflat, i, True)
        for j in range(COLS):
            first = flat[pl.ds(pl.multiple_of((i * COLS + j) * 16, 16), SUB)]
            gin[i, j] = (v[j] + first).astype(BF16)
        return 0

    lax.fori_loop(0, ROWS, line_back, 0)

    for c in up_z:
        c.wait_recv()
    v = up_q[z].astype(F32)
    for k in range(NZ - 1):
        v = v + up2[k].astype(F32)
    gup[core, yh, z] = v.astype(BF16)

    def up_to(where, cc, hh, zz, send, recv):
        ref = gup.at[cc, hh, zz]
        return remote(ref, ref, send, recv, where)

    def up_home(k):
        return lax.rem(z - k + NZ, NZ)

    ua = [up_to(zp[k], core, yh, z, ua_s.at[k], ua_r.at[k]) for k in range(NZ - 1)]
    uf = [up_to(far, core, yh, up_home(k), uf_s.at[k], uf_r.at[k]) for k in range(NZ)]
    ut = [up_to(twin, core, yh, up_home(k), ut_s.at[0, k], ut_r.at[0, k]) for k in range(NZ)]
    vt = [up_to(twin, core, 1 - yh, up_home(k), ut_s.at[1, k], ut_r.at[1, k]) for k in range(NZ)]
    for c in ua:
        c.start()
    uf[0].start()
    ut[0].start()
    down_far.wait_recv()
    gdown[core, z] = (down_c[...].astype(F32) + down2[...].astype(F32)).astype(BF16)

    def down_to(where, cc, zz, send, recv):
        ref = gdown.at[cc, zz]
        return remote(ref, ref, send, recv, where)

    da = [down_to(zp[k], core, z, da_s.at[k], da_r.at[k]) for k in range(NZ - 1)]
    dt = [down_to(twin, core, up_home(k), dt_s.at[k], dt_r.at[k]) for k in range(NZ)]
    for c in da:
        c.start()
    dt[0].start()

    for k in range(15):
        k2[k].wait_recv()
    v = ker_z_in[0].astype(F32)
    for k in range(1, 16):
        v = v + ker_z_in[k].astype(F32)
    ker_out[core, col] = v.astype(BF16)
    k4 = [
        remote(ker_out.at[core, col], ker_out.at[core, col], k4_s.at[k], k4_r.at[k], colp[k])
        for k in range(N_COL - 1)
    ]
    for c in k4:
        c.start()

    tok = at_home(part_at, part_xs, part_x, part_ys, part_y)
    lanes = lax.broadcasted_iota(jnp.int32, (SLOT_PAD, 256), 1)
    rows = lax.broadcasted_iota(jnp.int32, (SLOT_PAD, 256), 0)
    named = slots_row
    live = jnp.sum(jnp.where(lanes == rows + col * SLOT_PAD, named, 0.0), axis=1, keepdims=True)
    seq[...] = jnp.where(
        live[:SLOTS] > 0.5, tok[:SLOTS].astype(BF16).astype(F32), text[...].astype(F32)
    ).astype(BF16)

    for k in range(1, NZ):
        b = up_home(k)
        up_to(zp[k - 1], core, yh, b, ua_s.at[k - 1], ua_r.at[k - 1]).wait_recv()
        uf[k].start()
        ut[k].start()
    for k in range(N_COL - 1):
        b = ker_out.at[core, colf[k]]
        remote(b, b, k4_s.at[k], k4_r.at[k], colp[k]).wait_recv()
    k5 = remote(ker_out.at[core], ker_out.at[core], k5_s.at[0], k5_r.at[0], twin)
    k5.start()
    for k in range(1, NZ):
        b = up_home(k)
        down_to(zp[k - 1], core, b, da_s.at[k - 1], da_r.at[k - 1]).wait_recv()
        dt[k].start()
    b = ker_out.at[1 - core]
    remote(b, b, k5_s.at[0], k5_r.at[0], twin).wait_recv()
    for t in range(49):
        kflat[pl.ds(t * 16, SUB)] = ker_out[t % 2, t // 4, t // 2 % 2].astype(F32)
    for g in range(SUB):
        gker[:, g * LANE : (g + 1) * LANE] = kflat[pl.ds(g, 49, stride=16)]
    for k in range(NZ):
        up_to(far, core, 1 - yh, up_home(k), uf_s.at[k], uf_r.at[k]).wait_recv()
        vt[k].start()
    for k in range(NZ):
        b = up_home(k)
        up_to(twin, 1 - core, yh, b, ut_s.at[0, k], ut_r.at[0, k]).wait_recv()
        up_to(twin, 1 - core, 1 - yh, b, ut_s.at[1, k], ut_r.at[1, k]).wait_recv()
        down_to(twin, 1 - core, b, dt_s.at[k], dt_r.at[k]).wait_recv()
    for ref in (g_all, n_all):
        for c in own(*ref):
            c.wait_send()
        for dy in range(1, NY):
            for dx in range(1, NX):
                passed(*ref, dy, dx).wait_send()
    for c in f_halo + list(ng_xs.values()) + list(part_xs.values()) + ng_ys + part_ys + pair:
        c.wait_send()
    for c in halo + [up_far, down_far, k0, k5] + down_z + up_z + k1 + k2 + k4:
        c.wait_send()
    for c in ua + uf + ut + vt + da + dt:
        c.wait_send()


def whole(*operands):
    vm = pl.BlockSpec(memory_space=pltpu.VMEM)
    dma = pltpu.SemaphoreType.DMA
    v = pltpu.VMEM
    w = D // NZ // NC // 2
    h = HID // NZ // NC
    band = N_COL * PIX
    every = N_COL * SLOT_PAD
    map_ = (ROWS + 6, COLS + 6, SUB, LANE)
    return pl.pallas_call(
        whole_kernel,
        out_shape=(
            jax.ShapeDtypeStruct((SLOTS, D), BF16),
            jax.ShapeDtypeStruct((ROWS, COLS, SUB, LANE), BF16),
            jax.ShapeDtypeStruct((49, D), F32),
            jax.ShapeDtypeStruct((NC, 2, NZ, w, HID), BF16),
            jax.ShapeDtypeStruct((NC, NZ, h, D), BF16),
        ),
        in_specs=[vm] * 6
        + [pl.BlockSpec(memory_space=pltpu.SMEM), vm]
        + [pl.BlockSpec(memory_space=pl.ANY)] * 3,
        out_specs=[vm] * 5,
        scratch_shapes=[
            v((D, HID), BF16), v((HID, D), BF16), v((SLOTS, D), BF16), v((SLOT_PAD, D), F32),
            v(map_, BF16), v(map_, F32), v((PIX * 16, LANE), F32), v((49 * 16, LANE), F32),
            v((32, D), F32), v((PIX, D), F32),
            v((N_COL, PIX, D), BF16), v((band, D), BF16), v((every, D), BF16),
            v((band, every), BF16), v((band, D), BF16), v((32, D), F32),
            v((band, HID), F32), v((band, HID), BF16), v((band, HID), BF16),
            v((N_COL, PIX, D), BF16), v((NX - 1, NY, PIX, D), BF16),
            v((NY - 1, PIX, D), BF16), v((NY - 1, PIX, D), BF16),
            v((every, D), BF16), v((NX - 1, NY, SLOT_PAD, D), BF16),
            v((NY - 1, SLOT_PAD, D), BF16), v((NY - 1, SLOT_PAD, D), BF16),
            v((NC, 2, NZ, w, HID), BF16), v((NC, NZ, h, D), BF16),
            v((2, NZ, w, HID), BF16), v((NZ, h, D), BF16),
            v((NZ, w, HID), BF16), v((NZ - 1, h, D), BF16),
            v((NZ - 1, w, HID), BF16), v((h, D), BF16),
            v((2, NZ, w, HID), BF16), v((NZ, h, D), BF16),
            v((NZ, w, HID), BF16), v((h, D), BF16),
            v(map_, BF16), v((ROWS, COLS, SUB, LANE), F32),
            v((NC, 16, 2, SUB, LANE), BF16), v((16, 2, SUB, LANE), BF16),
            v((16, 2, SUB, LANE), BF16), v((15, 2, SUB, LANE), BF16),
            v((2, SUB, LANE), BF16), v((16, 2, SUB, LANE), BF16), v((NC, 16, 2, SUB, LANE), BF16),
            dma((3,)), dma((8,)), dma((8,)),
            dma((NY, NX)), dma((NY, NX)), dma((NY, NX)), dma((NY, NX)),
            dma((NX, NY)), dma((NX, NY)), dma((3,)), dma((3,)),
            dma((NX, NY)), dma((NX, NY)), dma((3,)), dma((3,)),
            dma((8,)), dma((8,)),
            dma((2,)), dma((2,)), dma((7,)), dma((7,)), dma((7,)), dma((7,)), dma((2,)), dma((2,)),
            dma((7,)), dma((7,)), dma((7,)), dma((7,)), dma((8,)), dma((8,)), dma((8,)), dma((8,)),
            dma((2, 8)), dma((2, 8)),
            dma((1,)), dma((1,)), dma((15,)), dma((15,)), dma((15,)), dma((15,)),
            dma((15,)), dma((15,)), dma((1,)), dma((1,)),
        ],
        compiler_params=pltpu.CompilerParams(
            collective_id=0, has_side_effects=True, vmem_limit_bytes=VMEM_LIMIT
        ),
    )(*operands)


def local(
    features, kernel, ln_gain, ln_bias, w_up, b_up, w_down, layer_scale,
    text_embed, slot_token, seq_grad,
):
    feat = features.reshape(ROWS, COLS, SUB, LANE)
    seq, gin, gker, gup, gdown = whole(
        feat, kernel, ln_gain, ln_bias, b_up, layer_scale, slot_token, seq_grad, w_up, w_down,
        text_embed,
    )
    return (
        seq, gin.reshape(ROWS, COLS, D), gker, gup.reshape(D, HID), gdown.reshape(HID, D),
    )


def solution(mesh):
    placed = (
        P("row", "col", None), P(), P(), P(), P(None, "col"), P("col"), P("col", None), P(),
        P(("row", "col"), None), P(("row", "col")), P(("row", "col"), None),
    )
    return jax.shard_map(
        local,
        mesh=mesh,
        in_specs=placed,
        out_specs=(
            P(("row", "col"), None), P("row", "col", None), P(), P(None, "col"), P("col", None),
        ),
        check_vma=False,
    )
```

```python
import jax
import jax.numpy as jnp
from jax import lax
from jax.experimental import pallas as pl
from jax.experimental.pallas import tpu as pltpu
from jax.sharding import PartitionSpec as P

F32, BF16 = jnp.float32, jnp.bfloat16
D, LANE, SUB = 1536, 128, 12
ROWS, COLS, PIX, SLOTS, SLOT_PAD = 4, 6, 24, 12, 16
N_ROW, N_COL = 32, 16
NX, NY = 4, 4
NZ, NC = 8, 2
HID = 256
DIRS = [(a, b) for a in (-1, 0, 1) for b in (-1, 0, 1) if (a, b) != (0, 0)]
MESH = pl.DeviceIdType.MESH
VMEM_LIMIT = 52000 * 1024
SRC_ROW = {1: (1, 3), 0: (0, 4), -1: (0, 3)}
DST_ROW = {1: 0, 0: 3, -1: 7}
SRC_COL = {1: (3, 3), 0: (0, 6), -1: (0, 3)}
DST_COL = {1: 0, 0: 3, -1: 9}


def remote(src, dst, send, recv, where):
    return pltpu.make_async_remote_copy(
        src_ref=src, dst_ref=dst, send_sem=send, recv_sem=recv, device_id=where, device_id_type=MESH
    )


def greet(where):
    barrier = pltpu.get_barrier_semaphore()
    for device in where:
        pl.semaphore_signal(barrier, inc=1, device_id=device, device_id_type=MESH)
    return barrier


def halo_copies(pad, row, col, send, recv):
    out = []
    for k, (a, b) in enumerate(DIRS):
        r0, nr = SRC_ROW[a]
        c0, nc = SRC_COL[b]
        where = (lax.rem(row + a + N_ROW, N_ROW), lax.rem(col + b + N_COL, N_COL))
        out.append(
            remote(
                pad.at[pl.ds(3 + r0, nr), pl.ds(3 + c0, nc)],
                pad.at[pl.ds(DST_ROW[a], nr), pl.ds(DST_COL[b], nc)],
                send.at[k],
                recv.at[k],
                where,
            )
        )
    return out


def widen(pad, wide, row, col):
    top = jnp.where(row == 0, 0.0, 1.0)
    bottom = jnp.where(row == N_ROW - 1, 0.0, 1.0)
    left = jnp.where(col == 0, 0.0, 1.0)
    right = jnp.where(col == N_COL - 1, 0.0, 1.0)
    for a in range(ROWS + 6):
        edge = top if a < 3 else bottom if a >= 7 else 1.0
        wide[a, pl.ds(0, 3)] = pad[a, pl.ds(0, 3)].astype(F32) * (edge * left)
        if a < 3 or a >= 7:
            wide[a, pl.ds(3, 6)] = pad[a, pl.ds(3, 6)].astype(F32) * edge
        else:
            wide[a, pl.ds(3, 6)] = pad[a, pl.ds(3, 6)].astype(F32)
        wide[a, pl.ds(9, 3)] = pad[a, pl.ds(9, 3)].astype(F32) * (edge * right)


def row_of_taps(wide, kern, i, flip):
    def step(p, acc):
        line = wide[i + (6 - p if flip else p)]
        for q in range(7):
            s = 6 - q if flip else q
            tap = kern[pl.ds(pl.multiple_of((p * 7 + q) * 16, 16), SUB)]
            acc = acc + line[s : s + COLS] * tap
        return acc

    return lax.fori_loop(0, 7, step, jnp.zeros((COLS, SUB, LANE), F32))


def dot(a, b, ca, cb):
    return lax.dot_general(a, b, (((ca,), (cb,)), ((), ())), preferred_element_type=F32)


def whole_kernel(
    feat, slot, seq_grad_hbm, kern_hbm, ln_gain_hbm, ln_bias_hbm, b_up_hbm, layer_scale_hbm,
    w_down_hbm, w_up_hbm, text_hbm,
    seq, gin, gker, gup, gdown,
    seq_grad, kern, ln_gain, ln_bias, b_up, layer_scale, w_down, w_up, text, block,
    pad, wide, flat, kflat, feat2, mixed, normed, band, every, select, bg, og, act_grad,
    act, pre_grad, ng, ng_x, ng_t, ng_y, part, part_x, part_t, part_y,
    up, down, up0, down0, up1, down1, up2, down2, up_h, down_h, up_q, down_c,
    mgpad, mwide, ker, ker_p, ker_h, ker_in, ker_z, ker_z_in, ker_out,
    w_s, f_s, f_r, n_s, n_r, g_s, g_r,
    nx_s, nx_r, ny_s, ny_r, px_s, px_r, py_s, py_r, halo_s, halo_r,
    c_s, c_r, dz_s, dz_r, uz_s, uz_r, h_s, h_r,
    da_s, da_r, ua_s, ua_r, uf_s, uf_r, dt_s, dt_r, ut_s, ut_r,
    k0_s, k0_r, k1_s, k1_r, k2_s, k2_r, k4_s, k4_r, k5_s, k5_r,
):
    row, col = lax.axis_index("row"), lax.axis_index("col")
    y, x = col // NX, lax.rem(col, NX)
    core = lax.rem(row, NC)
    z = lax.rem(row // NC, NZ)
    yh = row // (NC * NZ)
    at = lambda yy, zz, cc: ((yy * NZ + zz) * NC + cc, col)
    peer = lambda dy, dx: lax.rem(y + dy + NY, NY) * NX + lax.rem(x + dx + NX, NX)
    yp = [(row, peer(dy, 0)) for dy in range(1, NY)]
    xp = [(row, peer(0, dx)) for dx in range(1, NX)]
    colp = [(row, lax.rem(col + k, N_COL)) for k in range(1, N_COL)]
    colb = [lax.rem(col + k, N_COL) for k in range(1, N_COL)]
    colf = [lax.rem(col - k + N_COL, N_COL) for k in range(1, N_COL)]
    zb = [lax.rem(z + k, NZ) for k in range(1, NZ)]
    zf = [lax.rem(z - k + NZ, NZ) for k in range(1, NZ)]
    zp = [at(yh, k, core) for k in zb]
    twin = at(yh, z, 1 - core)
    far = at(1 - yh, z, core)
    rowp = zp + [at(1 - yh, lax.rem(z + k, NZ), core) for k in range(NZ)]
    around = [
        (lax.rem(row + a + N_ROW, N_ROW), lax.rem(col + b + N_COL, N_COL)) for a, b in DIRS
    ]
    held_in = (seq_grad, kern, ln_gain, ln_bias, b_up, layer_scale, w_down, w_up, text)
    from_hbm = (
        seq_grad_hbm, kern_hbm, ln_gain_hbm, ln_bias_hbm, b_up_hbm, layer_scale_hbm,
        w_down_hbm, w_up_hbm, text_hbm,
    )
    fetch = [
        pltpu.make_async_copy(a, b, w_s.at[k]) for k, (a, b) in enumerate(zip(from_hbm, held_in))
    ]
    for c in fetch:
        c.start()
    slot_rows = lambda d: pl.ds(pl.multiple_of(d * SLOT_PAD, SLOT_PAD), SLOT_PAD)

    partners = around + colp + rowp + [twin]
    barrier = greet(partners)
    pad[pl.ds(3, ROWS), pl.ds(3, COLS)] = feat[...]
    lane = lax.broadcasted_iota(jnp.int32, (1, 256), 1)
    name = jnp.zeros((1, 256), jnp.int32)
    for r in range(SLOTS):
        name = jnp.where(lane == col * SLOT_PAD + r, slot[r] + 1, name)
    block[...] = jnp.zeros_like(block)
    fetch[0].wait()
    block[pl.ds(0, SLOTS)] = seq_grad[...].astype(F32)
    block[pl.ds(SLOTS, 1), pl.ds(0, 256)] = name.astype(F32)
    every[slot_rows(col)] = block[...].astype(BF16)
    pl.semaphore_wait(barrier, len(partners))

    f_halo = halo_copies(pad, row, col, f_s, f_r)
    for c in f_halo:
        c.start()

    n_at = lambda d: normed.at[d]
    g_at = lambda d: every.at[slot_rows(d)]

    def own(at_, send, recv):
        out = []
        for dy in range(1, NY):
            out.append(remote(at_(col), at_(col), send.at[dy, 0], recv.at[dy, 0], yp[dy - 1]))
        for dx in range(1, NX):
            out.append(remote(at_(col), at_(col), send.at[0, dx], recv.at[0, dx], xp[dx - 1]))
        return out

    def passed(at_, send, recv, dy, dx):
        b = peer(-dy, 0)
        return remote(at_(b), at_(b), send.at[dy, dx], recv.at[dy, dx], xp[dx - 1])

    def came(at_, send, recv, dy, dx):
        b = peer(-dy, -dx)
        return remote(at_(b), at_(b), send.at[dy, dx], recv.at[dy, dx], (row, peer(dy, dx)))

    g_all, n_all = (g_at, g_s, g_r), (n_at, n_s, n_r)

    def onward(ref):
        for a in range(1, 4):
            came(*ref, a, 0).wait_recv()
            for b in range(1, 4):
                passed(*ref, a, b).start()

    def arrived(ref):
        for a in range(4):
            for b in range(1, 4):
                came(*ref, a, b).wait_recv()

    for c in own(*g_all):
        c.start()
    for c in fetch[1:6]:
        c.wait()
    gain, bias = ln_gain[...].reshape(1, D), ln_bias[...].reshape(1, D)
    b_row = b_up[...].reshape(1, HID)
    for g in range(SUB):
        kflat[pl.ds(g, 49, stride=16)] = kern[:, g * LANE : (g + 1) * LANE]
    for i in range(ROWS):
        for j in range(COLS):
            flat[pl.ds((i * COLS + j) * 16, SUB)] = feat[i, j].astype(F32)
    feat2[...] = jnp.zeros_like(feat2)
    for g in range(SUB):
        feat2[pl.ds(0, PIX), pl.ds(g * LANE, LANE)] = flat[pl.ds(g, PIX, stride=16)]
    for c in f_halo:
        c.wait_recv()
    onward(g_all)
    widen(pad, wide, row, col)

    def line(i, _):
        acc = row_of_taps(wide, kflat, i, False)
        for j in range(COLS):
            flat[pl.ds(pl.multiple_of((i * COLS + j) * 16, 16), SUB)] = acc[j]
        return 0

    lax.fori_loop(0, ROWS, line, 0)
    for g in range(SUB):
        mixed[:, pl.ds(g * LANE, LANE)] = flat[pl.ds(g, PIX, stride=16)]
    m = mixed[...]
    centred = m - jnp.mean(m, axis=-1, keepdims=True)
    var = jnp.mean(centred * centred, axis=-1, keepdims=True)
    normed[col] = (centred * lax.rsqrt(var + 1e-06) * gain + bias).astype(BF16)
    for c in own(*n_all):
        c.start()
    onward(n_all)

    arrived(g_all)
    slots_row = name.astype(F32)
    names = jnp.zeros((SLOT_PAD, 256), F32)
    for d in range(N_COL):
        names = names + every[pl.ds(d * SLOT_PAD, SLOT_PAD), pl.ds(0, 256)].astype(F32)
    names = names[SLOTS : SLOTS + 1] - 1.0

    def token_of(count, first):
        p = lax.broadcasted_iota(jnp.int32, (count, 1), 0)
        d = jnp.where(p >= PIX, 1, 0)
        p = p - d * PIX
        one = lambda c: jnp.where(c, 1, 0)
        i = one(p >= 6) + one(p >= 12) + one(p >= 18)
        j = p - i * COLS
        t = 3 * one(i >= 2) + one(j >= 2) + one(j >= 4)
        return ((first + d) * 6 + t).astype(F32)

    for d in range(0, N_COL, 2):
        hit = token_of(2 * PIX, d) == names
        select[pl.ds(d * PIX, 2 * PIX)] = jnp.where(hit, 1.0, 0.0).astype(BF16)
    p32 = lax.broadcasted_iota(jnp.int32, (32, 1), 0)
    hit = jnp.where(p32 < PIX, token_of(32, col), -9.0) == names
    mine = jnp.where(hit, 1.0, 0.0).astype(BF16)

    def grads(c, _):
        cut = pl.ds(pl.multiple_of(c * 512, 512), 512)
        g = dot(select[...], every[:, cut], 1, 0) * 0.25
        bg[:, cut] = (g * layer_scale[cut].reshape(1, 512)).astype(BF16)
        og[:, cut] = dot(mine, every[:, cut], 1, 0) * 0.25
        return 0

    for c in fetch[6:]:
        c.wait()
    lax.fori_loop(0, 3, grads, 0)

    def hidden_grads(r, _):
        cut = pl.ds(pl.multiple_of(r * 128, 128), 128)
        act_grad[cut] = dot(bg[cut], w_down[...], 1, 1)
        return 0

    lax.fori_loop(0, 3, hidden_grads, 0)

    arrived(n_all)
    for d in range(0, N_COL, 2):
        two = jnp.concatenate([normed[d].astype(F32), normed[d + 1].astype(F32)], axis=0)
        band[pl.ds(d * PIX, 2 * PIX)] = two.astype(BF16)

    def hidden(r, _):
        cut = pl.ds(pl.multiple_of(r * 128, 128), 128)
        v = dot(band[cut], w_up[...], 1, 0) + b_row
        k0, k1 = 0.7978845608028654, 0.044715
        t = jnp.tanh(k0 * (v + k1 * v * v * v))
        act[cut] = (0.5 * v * (1.0 + t)).astype(BF16)
        slope = 0.5 * (1.0 + t) + 0.5 * v * (1.0 - t * t) * (k0 * (1.0 + 3.0 * k1 * v * v))
        pre_grad[cut] = (act_grad[cut] * slope).astype(BF16)
        return 0

    lax.fori_loop(0, 3, hidden, 0)

    def back(c, _):
        cut = pl.ds(pl.multiple_of(c * 512, 512), 512)
        v = dot(pre_grad[...], w_up[cut], 1, 1)
        for d in range(N_COL):
            ng[d, :, cut] = v[d * PIX : (d + 1) * PIX].astype(BF16)
        return 0

    lax.fori_loop(0, 3, back, 0)

    def across_x(at_, to, send, recv):
        out = {}
        for dy in (1, 2, 3, 0):
            for dx in range(1, NX):
                out[dy, dx] = remote(
                    at_(peer(dy, dx)), to.at[dx - 1, dy], send.at[dx, dy], recv.at[dx, dy],
                    xp[dx - 1],
                )
        return out

    def along_y(at_, xs, came_x, held, to, send, recv):
        out = []
        for dy in range(1, NY):
            v = at_(peer(dy, 0))[...].astype(F32)
            for dx in range(1, NX):
                xs[dy, dx].wait_recv()
                v = v + came_x[dx - 1, dy].astype(F32)
            held[dy - 1] = v.astype(BF16)
            out.append(
                remote(held.at[dy - 1], to.at[dy - 1], send.at[dy - 1], recv.at[dy - 1], yp[dy - 1])
            )
            out[-1].start()
        return out

    def at_home(at_, xs, came_x, ys, came_y):
        v = at_(col)[...].astype(F32)
        for dx in range(1, NX):
            xs[0, dx].wait_recv()
            v = v + came_x[dx - 1, 0].astype(F32)
        for dy in range(1, NY):
            ys[dy - 1].wait_recv()
            v = v + came_y[dy - 1].astype(F32)
        return v

    ng_at = lambda d: ng.at[d]
    ng_xs = across_x(ng_at, ng_x, nx_s, nx_r)
    for c in ng_xs.values():
        c.start()

    def down_part(c, _):
        cut = pl.ds(pl.multiple_of(c * 512, 512), 512)
        v = dot(act[...], bg[:, cut], 0, 0)
        for k in range(NC * NZ):
            down[k // NZ, k % NZ, :, cut] = v[k * 16 : (k + 1) * 16].astype(BF16)
        return 0

    lax.fori_loop(0, 3, down_part, 0)
    pair = [
        remote(down.at[1 - core], down0, c_s.at[0], c_r.at[0], twin),
        remote(up.at[1 - core], up0, c_s.at[1], c_r.at[1], twin),
    ]
    pair[0].start()
    for c in range(4):
        v = dot(band[:, c * 384 : (c + 1) * 384], pre_grad[...], 0, 0)
        for k in range(8):
            up[c // 2, c % 2, k] = v[k * 48 : (k + 1) * 48].astype(BF16)
    pair[1].start()

    pooled = (dot(select[...], act[...], 0, 0) * 0.25).astype(BF16)

    def tokens(c, _):
        cut = pl.ds(pl.multiple_of(c * 512, 512), 512)
        v = dot(pooled, w_down[:, cut], 1, 0) * layer_scale[cut].reshape(1, 512)
        v = v + 0.25 * dot(mine, feat2[:, cut].astype(BF16), 0, 0)
        part[:, cut] = v.astype(BF16)
        return 0

    lax.fori_loop(0, 3, tokens, 0)
    part_at = lambda d: part.at[slot_rows(d)]
    part_xs = across_x(part_at, part_x, px_s, px_r)

    for c in pair:
        c.wait_recv()
    for k in range(NZ):
        down_h[k] = (down[core, k].astype(F32) + down0[k].astype(F32)).astype(BF16)
        for n in range(2):
            up_h[n, k] = (up[core, n, k].astype(F32) + up0[n, k].astype(F32)).astype(BF16)
    up_far = remote(up_h.at[1 - yh], up1, h_s.at[0], h_r.at[0], far)
    up_far.start()
    down_z = [
        remote(down_h.at[zb[k]], down1.at[k], dz_s.at[k], dz_r.at[k], zp[k]) for k in range(NZ - 1)
    ]
    for c in down_z:
        c.start()

    ng_ys = along_y(ng_at, ng_xs, ng_x, ng_t, ng_y, ny_s, ny_r)
    for c in part_xs.values():
        c.start()
    total = at_home(ng_at, ng_xs, ng_x, ng_ys, ng_y)
    m = mixed[...]
    centred = m - jnp.mean(m, axis=-1, keepdims=True)
    inv = lax.rsqrt(jnp.mean(centred * centred, axis=-1, keepdims=True) + 1e-06)
    hat = centred * inv
    dy_ = total * gain
    dm = inv * (
        dy_
        - jnp.mean(dy_, axis=-1, keepdims=True)
        - hat * jnp.mean(dy_ * hat, axis=-1, keepdims=True)
    )
    dm = dm.astype(BF16).astype(F32)
    for g in range(SUB):
        flat[pl.ds(g, PIX, stride=16)] = dm[:, g * LANE : (g + 1) * LANE]
    for i in range(ROWS):
        for j in range(COLS):
            v = flat[pl.ds((i * COLS + j) * 16, SUB)]
            mgpad[3 + i, 3 + j] = v.astype(BF16)
            mwide[i, j] = v
    halo = halo_copies(mgpad, row, col, halo_s, halo_r)
    for c in halo:
        c.start()

    def taps(p, _):
        acc = [jnp.zeros((SUB, LANE), F32) for _ in range(7)]
        for i in range(ROWS):
            line = wide[i + p]
            own_line = mwide[i]
            for q in range(7):
                acc[q] = acc[q] + jnp.sum(line[q : q + COLS] * own_line, axis=0)
        for q in range(7):
            t = p * 7 + q
            ker[lax.rem(t, 2), t // 4, lax.rem(t // 2, 2)] = acc[q].astype(BF16)
        return 0

    lax.fori_loop(0, 7, taps, 0)
    for t in range(49, 64):
        ker[t % 2, t // 4, t // 2 % 2] = jnp.zeros((SUB, LANE), BF16)
    k0 = remote(ker.at[1 - core], ker_p, k0_s.at[0], k0_r.at[0], twin)
    k0.start()

    k0.wait_recv()
    for k in range(16):
        ker_h[k] = (ker[core, k].astype(F32) + ker_p[k].astype(F32)).astype(BF16)
    k1 = [
        remote(ker_h.at[colb[k]], ker_in.at[k], k1_s.at[k], k1_r.at[k], colp[k])
        for k in range(N_COL - 1)
    ]
    for c in k1:
        c.start()
    for c in down_z:
        c.wait_recv()
    v = down_h[z].astype(F32)
    for k in range(NZ - 1):
        v = v + down1[k].astype(F32)
    down_c[...] = v.astype(BF16)
    down_far = remote(down_c, down2, h_s.at[1], h_r.at[1], far)
    down_far.start()
    up_far.wait_recv()
    for k in range(NZ):
        up_q[k] = (up_h[yh, k].astype(F32) + up1[k].astype(F32)).astype(BF16)
    up_z = [
        remote(up_q.at[zb[k]], up2.at[k], uz_s.at[k], uz_r.at[k], zp[k]) for k in range(NZ - 1)
    ]
    for c in up_z:
        c.start()

    part_ys = along_y(part_at, part_xs, part_x, part_t, part_y, py_s, py_r)

    for c in k1:
        c.wait_recv()
    v = ker_h[col].astype(F32)
    for k in range(N_COL - 1):
        v = v + ker_in[k].astype(F32)
    ker_z[...] = v.astype(BF16)
    place = yh * NZ + z
    ker_z_in[place] = ker_z[...]
    k2 = [
        remote(ker_z, ker_z_in.at[place], k2_s.at[k], k2_r.at[k], rowp[k]) for k in range(15)
    ]
    for c in k2:
        c.start()

    for c in halo:
        c.wait_recv()
    widen(mgpad, wide, row, col)
    for g in range(SUB):
        flat[pl.ds(g, PIX, stride=16)] = og[pl.ds(0, PIX), pl.ds(g * LANE, LANE)]

    def line_back(i, _):
        v = row_of_taps(wide, kflat, i, True)
        for j in range(COLS):
            first = flat[pl.ds(pl.multiple_of((i * COLS + j) * 16, 16), SUB)]
            gin[i, j] = (v[j] + first).astype(BF16)
        return 0

    lax.fori_loop(0, ROWS, line_back, 0)

    for c in up_z:
        c.wait_recv()
    v = up_q[z].astype(F32)
    for k in range(NZ - 1):
        v = v + up2[k].astype(F32)
    gup[core, yh, z] = v.astype(BF16)

    def up_to(where, cc, hh, zz, send, recv):
        ref = gup.at[cc, hh, zz]
        return remote(ref, ref, send, recv, where)

    def up_home(k):
        return lax.rem(z - k + NZ, NZ)

    ua = [up_to(zp[k], core, yh, z, ua_s.at[k], ua_r.at[k]) for k in range(NZ - 1)]
    uf = [up_to(far, core, yh, up_home(k), uf_s.at[k], uf_r.at[k]) for k in range(NZ)]
    ut = [up_to(twin, core, yh, up_home(k), ut_s.at[0, k], ut_r.at[0, k]) for k in range(NZ)]
    vt = [up_to(twin, core, 1 - yh, up_home(k), ut_s.at[1, k], ut_r.at[1, k]) for k in range(NZ)]
    for c in ua:
        c.start()
    uf[0].start()
    ut[0].start()
    down_far.wait_recv()
    gdown[core, z] = (down_c[...].astype(F32) + down2[...].astype(F32)).astype(BF16)

    def down_to(where, cc, zz, send, recv):
        ref = gdown.at[cc, zz]
        return remote(ref, ref, send, recv, where)

    da = [down_to(zp[k], core, z, da_s.at[k], da_r.at[k]) for k in range(NZ - 1)]
    dt = [down_to(twin, core, up_home(k), dt_s.at[k], dt_r.at[k]) for k in range(NZ)]
    for c in da:
        c.start()
    dt[0].start()

    for k in range(15):
        k2[k].wait_recv()
    v = ker_z_in[0].astype(F32)
    for k in range(1, 16):
        v = v + ker_z_in[k].astype(F32)
    ker_out[core, col] = v.astype(BF16)
    k4 = [
        remote(ker_out.at[core, col], ker_out.at[core, col], k4_s.at[k], k4_r.at[k], colp[k])
        for k in range(N_COL - 1)
    ]
    for c in k4:
        c.start()

    tok = at_home(part_at, part_xs, part_x, part_ys, part_y)
    lanes = lax.broadcasted_iota(jnp.int32, (SLOT_PAD, 256), 1)
    rows = lax.broadcasted_iota(jnp.int32, (SLOT_PAD, 256), 0)
    named = slots_row
    live = jnp.sum(jnp.where(lanes == rows + col * SLOT_PAD, named, 0.0), axis=1, keepdims=True)
    seq[...] = jnp.where(
        live[:SLOTS] > 0.5, tok[:SLOTS].astype(BF16).astype(F32), text[...].astype(F32)
    ).astype(BF16)

    for k in range(1, NZ):
        b = up_home(k)
        up_to(zp[k - 1], core, yh, b, ua_s.at[k - 1], ua_r.at[k - 1]).wait_recv()
        uf[k].start()
        ut[k].start()
    for k in range(N_COL - 1):
        b = ker_out.at[core, colf[k]]
        remote(b, b, k4_s.at[k], k4_r.at[k], colp[k]).wait_recv()
    k5 = remote(ker_out.at[core], ker_out.at[core], k5_s.at[0], k5_r.at[0], twin)
    k5.start()
    for k in range(1, NZ):
        b = up_home(k)
        down_to(zp[k - 1], core, b, da_s.at[k - 1], da_r.at[k - 1]).wait_recv()
        dt[k].start()
    b = ker_out.at[1 - core]
    remote(b, b, k5_s.at[0], k5_r.at[0], twin).wait_recv()
    for t in range(49):
        kflat[pl.ds(t * 16, SUB)] = ker_out[t % 2, t // 4, t // 2 % 2].astype(F32)
    for g in range(SUB):
        gker[:, g * LANE : (g + 1) * LANE] = kflat[pl.ds(g, 49, stride=16)]
    for k in range(NZ):
        up_to(far, core, 1 - yh, up_home(k), uf_s.at[k], uf_r.at[k]).wait_recv()
        vt[k].start()
    for k in range(NZ):
        b = up_home(k)
        up_to(twin, 1 - core, yh, b, ut_s.at[0, k], ut_r.at[0, k]).wait_recv()
        up_to(twin, 1 - core, 1 - yh, b, ut_s.at[1, k], ut_r.at[1, k]).wait_recv()
        down_to(twin, 1 - core, b, dt_s.at[k], dt_r.at[k]).wait_recv()
    for ref in (g_all, n_all):
        for c in own(*ref):
            c.wait_send()
        for dy in range(1, NY):
            for dx in range(1, NX):
                passed(*ref, dy, dx).wait_send()
    for c in f_halo + list(ng_xs.values()) + list(part_xs.values()) + ng_ys + part_ys + pair:
        c.wait_send()
    for c in halo + [up_far, down_far, k0, k5] + down_z + up_z + k1 + k2 + k4:
        c.wait_send()
    for c in ua + uf + ut + vt + da + dt:
        c.wait_send()


def whole(*operands):
    vm = pl.BlockSpec(memory_space=pltpu.VMEM)
    dma = pltpu.SemaphoreType.DMA
    v = pltpu.VMEM
    w = D // NZ // NC // 2
    h = HID // NZ // NC
    band = N_COL * PIX
    every = N_COL * SLOT_PAD
    map_ = (ROWS + 6, COLS + 6, SUB, LANE)
    return pl.pallas_call(
        whole_kernel,
        out_shape=(
            jax.ShapeDtypeStruct((SLOTS, D), BF16),
            jax.ShapeDtypeStruct((ROWS, COLS, SUB, LANE), BF16),
            jax.ShapeDtypeStruct((49, D), F32),
            jax.ShapeDtypeStruct((NC, 2, NZ, w, HID), BF16),
            jax.ShapeDtypeStruct((NC, NZ, h, D), BF16),
        ),
        in_specs=[vm, pl.BlockSpec(memory_space=pltpu.SMEM)]
        + [pl.BlockSpec(memory_space=pltpu.HBM)] * 9,
        out_specs=[vm] * 5,
        scratch_shapes=[
            v((SLOTS, D), BF16), v((49, D), F32), v((D,), F32), v((D,), F32), v((HID,), F32),
            v((D,), F32), v((HID, D), BF16), v((D, HID), BF16), v((SLOTS, D), BF16),
            v((SLOT_PAD, D), F32),
            v(map_, BF16), v(map_, F32), v((PIX * 16, LANE), F32), v((49 * 16, LANE), F32),
            v((32, D), F32), v((PIX, D), F32),
            v((N_COL, PIX, D), BF16), v((band, D), BF16), v((every, D), BF16),
            v((band, every), BF16), v((band, D), BF16), v((32, D), F32),
            v((band, HID), F32), v((band, HID), BF16), v((band, HID), BF16),
            v((N_COL, PIX, D), BF16), v((NX - 1, NY, PIX, D), BF16),
            v((NY - 1, PIX, D), BF16), v((NY - 1, PIX, D), BF16),
            v((every, D), BF16), v((NX - 1, NY, SLOT_PAD, D), BF16),
            v((NY - 1, SLOT_PAD, D), BF16), v((NY - 1, SLOT_PAD, D), BF16),
            v((NC, 2, NZ, w, HID), BF16), v((NC, NZ, h, D), BF16),
            v((2, NZ, w, HID), BF16), v((NZ, h, D), BF16),
            v((NZ, w, HID), BF16), v((NZ - 1, h, D), BF16),
            v((NZ - 1, w, HID), BF16), v((h, D), BF16),
            v((2, NZ, w, HID), BF16), v((NZ, h, D), BF16),
            v((NZ, w, HID), BF16), v((h, D), BF16),
            v(map_, BF16), v((ROWS, COLS, SUB, LANE), F32),
            v((NC, 16, 2, SUB, LANE), BF16), v((16, 2, SUB, LANE), BF16),
            v((16, 2, SUB, LANE), BF16), v((15, 2, SUB, LANE), BF16),
            v((2, SUB, LANE), BF16), v((16, 2, SUB, LANE), BF16), v((NC, 16, 2, SUB, LANE), BF16),
            dma((9,)), dma((8,)), dma((8,)),
            dma((NY, NX)), dma((NY, NX)), dma((NY, NX)), dma((NY, NX)),
            dma((NX, NY)), dma((NX, NY)), dma((3,)), dma((3,)),
            dma((NX, NY)), dma((NX, NY)), dma((3,)), dma((3,)),
            dma((8,)), dma((8,)),
            dma((2,)), dma((2,)), dma((7,)), dma((7,)), dma((7,)), dma((7,)), dma((2,)), dma((2,)),
            dma((7,)), dma((7,)), dma((7,)), dma((7,)), dma((8,)), dma((8,)), dma((8,)), dma((8,)),
            dma((2, 8)), dma((2, 8)),
            dma((1,)), dma((1,)), dma((15,)), dma((15,)), dma((15,)), dma((15,)),
            dma((15,)), dma((15,)), dma((1,)), dma((1,)),
        ],
        compiler_params=pltpu.CompilerParams(
            collective_id=0, has_side_effects=True, vmem_limit_bytes=VMEM_LIMIT
        ),
    )(*operands)


def local(
    features, kernel, ln_gain, ln_bias, w_up, b_up, w_down, layer_scale,
    text_embed, slot_token, seq_grad,
):
    feat = features.reshape(ROWS, COLS, SUB, LANE)
    seq, gin, gker, gup, gdown = whole(
        feat, slot_token, seq_grad, kernel, ln_gain, ln_bias, b_up, layer_scale, w_down, w_up,
        text_embed,
    )
    return (
        seq, gin.reshape(ROWS, COLS, D), gker, gup.reshape(D, HID), gdown.reshape(HID, D),
    )


def solution(mesh):
    placed = (
        P("row", "col", None), P(), P(), P(), P(None, "col"), P("col"), P("col", None), P(),
        P(("row", "col"), None), P(("row", "col")), P(("row", "col"), None),
    )
    return jax.shard_map(
        local,
        mesh=mesh,
        in_specs=placed,
        out_specs=(
            P(("row", "col"), None), P("row", "col", None), P(), P(None, "col"), P("col", None),
        ),
        check_vma=False,
    )
```

```python
import jax
import jax.numpy as jnp
from jax import lax
from jax.experimental import pallas as pl
from jax.experimental.pallas import tpu as pltpu
from jax.sharding import PartitionSpec as P

F32, BF16 = jnp.float32, jnp.bfloat16
D, LANE, SUB = 1536, 128, 12
ROWS, COLS, PIX, SLOTS, SLOT_PAD = 4, 6, 24, 12, 16
N_ROW, N_COL = 32, 16
NX, NY = 4, 4
NZ, NC = 8, 2
HID = 256
DIRS = [(a, b) for a in (-1, 0, 1) for b in (-1, 0, 1) if (a, b) != (0, 0)]
MESH = pl.DeviceIdType.MESH
VMEM_LIMIT = 52000 * 1024
SRC_ROW = {1: (1, 3), 0: (0, 4), -1: (0, 3)}
DST_ROW = {1: 0, 0: 3, -1: 7}
SRC_COL = {1: (3, 3), 0: (0, 6), -1: (0, 3)}
DST_COL = {1: 0, 0: 3, -1: 9}


def remote(src, dst, send, recv, where):
    return pltpu.make_async_remote_copy(
        src_ref=src, dst_ref=dst, send_sem=send, recv_sem=recv, device_id=where, device_id_type=MESH
    )


def greet(where):
    barrier = pltpu.get_barrier_semaphore()
    for device in where:
        pl.semaphore_signal(barrier, inc=1, device_id=device, device_id_type=MESH)
    return barrier


def halo_copies(pad, row, col, send, recv):
    out = []
    for k, (a, b) in enumerate(DIRS):
        r0, nr = SRC_ROW[a]
        c0, nc = SRC_COL[b]
        where = (lax.rem(row + a + N_ROW, N_ROW), lax.rem(col + b + N_COL, N_COL))
        out.append(
            remote(
                pad.at[pl.ds(3 + r0, nr), pl.ds(3 + c0, nc)],
                pad.at[pl.ds(DST_ROW[a], nr), pl.ds(DST_COL[b], nc)],
                send.at[k],
                recv.at[k],
                where,
            )
        )
    return out


def widen(pad, wide, row, col):
    top = jnp.where(row == 0, 0.0, 1.0)
    bottom = jnp.where(row == N_ROW - 1, 0.0, 1.0)
    left = jnp.where(col == 0, 0.0, 1.0)
    right = jnp.where(col == N_COL - 1, 0.0, 1.0)
    for a in range(ROWS + 6):
        edge = top if a < 3 else bottom if a >= 7 else 1.0
        wide[a, pl.ds(0, 3)] = pad[a, pl.ds(0, 3)].astype(F32) * (edge * left)
        if a < 3 or a >= 7:
            wide[a, pl.ds(3, 6)] = pad[a, pl.ds(3, 6)].astype(F32) * edge
        else:
            wide[a, pl.ds(3, 6)] = pad[a, pl.ds(3, 6)].astype(F32)
        wide[a, pl.ds(9, 3)] = pad[a, pl.ds(9, 3)].astype(F32) * (edge * right)


def row_of_taps(wide, kern, i, flip):
    def step(p, acc):
        line = wide[i + (6 - p if flip else p)]
        for q in range(7):
            s = 6 - q if flip else q
            tap = kern[pl.ds(pl.multiple_of((p * 7 + q) * 16, 16), SUB)]
            acc = acc + line[s : s + COLS] * tap
        return acc

    return lax.fori_loop(0, 7, step, jnp.zeros((COLS, SUB, LANE), F32))


def dot(a, b, ca, cb):
    return lax.dot_general(a, b, (((ca,), (cb,)), ((), ())), preferred_element_type=F32)


def whole_kernel(
    feat, slot, seq_grad_hbm, kern_hbm, ln_gain_hbm, ln_bias_hbm, b_up_hbm, layer_scale_hbm,
    w_down_hbm, w_up_hbm, text_hbm,
    seq, gin, gker, gup, gdown,
    seq_grad, kern, ln_gain, ln_bias, b_up, layer_scale, w_down, w_up, text, block,
    pad, wide, flat, kflat, feat2, mixed, normed, band, every, select, bg, og, act_grad,
    act, pre_grad, ng, ng_x, ng_t, ng_y, part, part_x, part_t, part_y,
    up, down, up0, down0, up1, down1, up2, down2, up_h, down_h, up_q, down_c,
    mgpad, mwide, ker, ker_p, ker_h, ker_in, ker_z, ker_z_in, ker_out,
    w_s, f_s, f_r, n_s, n_r, g_s, g_r,
    nx_s, nx_r, ny_s, ny_r, px_s, px_r, py_s, py_r, halo_s, halo_r,
    c_s, c_r, dz_s, dz_r, uz_s, uz_r, h_s, h_r,
    da_s, da_r, ua_s, ua_r, uf_s, uf_r, dt_s, dt_r, ut_s, ut_r,
    k0_s, k0_r, k1_s, k1_r, k2_s, k2_r, k4_s, k4_r, k5_s, k5_r,
):
    row, col = lax.axis_index("row"), lax.axis_index("col")
    y, x = col // NX, lax.rem(col, NX)
    core = lax.rem(row, NC)
    z = lax.rem(row // NC, NZ)
    yh = row // (NC * NZ)
    at = lambda yy, zz, cc: ((yy * NZ + zz) * NC + cc, col)
    peer = lambda dy, dx: lax.rem(y + dy + NY, NY) * NX + lax.rem(x + dx + NX, NX)
    yp = [(row, peer(dy, 0)) for dy in range(1, NY)]
    xp = [(row, peer(0, dx)) for dx in range(1, NX)]
    colp = [(row, lax.rem(col + k, N_COL)) for k in range(1, N_COL)]
    colb = [lax.rem(col + k, N_COL) for k in range(1, N_COL)]
    colf = [lax.rem(col - k + N_COL, N_COL) for k in range(1, N_COL)]
    zb = [lax.rem(z + k, NZ) for k in range(1, NZ)]
    zf = [lax.rem(z - k + NZ, NZ) for k in range(1, NZ)]
    zp = [at(yh, k, core) for k in zb]
    twin = at(yh, z, 1 - core)
    far = at(1 - yh, z, core)
    rowp = zp + [at(1 - yh, lax.rem(z + k, NZ), core) for k in range(NZ)]
    around = [
        (lax.rem(row + a + N_ROW, N_ROW), lax.rem(col + b + N_COL, N_COL)) for a, b in DIRS
    ]
    held_in = (seq_grad, kern, ln_gain, ln_bias, b_up, layer_scale, w_down, w_up, text)
    from_hbm = (
        seq_grad_hbm, kern_hbm, ln_gain_hbm, ln_bias_hbm, b_up_hbm, layer_scale_hbm,
        w_down_hbm, w_up_hbm, text_hbm,
    )
    fetch = [
        pltpu.make_async_copy(a, b, w_s.at[k]) for k, (a, b) in enumerate(zip(from_hbm, held_in))
    ]
    for c in fetch:
        c.start()
    slot_rows = lambda d: pl.ds(pl.multiple_of(d * SLOT_PAD, SLOT_PAD), SLOT_PAD)

    partners = around + colp + rowp + [twin]
    barrier = greet(partners)
    pad[pl.ds(3, ROWS), pl.ds(3, COLS)] = feat[...]
    lane = lax.broadcasted_iota(jnp.int32, (1, 256), 1)
    name = jnp.zeros((1, 256), jnp.int32)
    for r in range(SLOTS):
        name = jnp.where(lane == col * SLOT_PAD + r, slot[r] + 1, name)
    block[...] = jnp.zeros_like(block)
    fetch[0].wait()
    block[pl.ds(0, SLOTS)] = seq_grad[...].astype(F32)
    block[pl.ds(SLOTS, 1), pl.ds(0, 256)] = name.astype(F32)
    every[slot_rows(col)] = block[...].astype(BF16)
    pl.semaphore_wait(barrier, len(partners))

    f_halo = halo_copies(pad, row, col, f_s, f_r)
    for c in f_halo:
        c.start()

    n_at = lambda d: normed.at[d]
    g_at = lambda d: every.at[slot_rows(d)]

    def own(at_, send, recv):
        out = []
        for dy in range(1, NY):
            out.append(remote(at_(col), at_(col), send.at[dy, 0], recv.at[dy, 0], yp[dy - 1]))
        for dx in range(1, NX):
            out.append(remote(at_(col), at_(col), send.at[0, dx], recv.at[0, dx], xp[dx - 1]))
        return out

    def passed(at_, send, recv, dy, dx):
        b = peer(-dy, 0)
        return remote(at_(b), at_(b), send.at[dy, dx], recv.at[dy, dx], xp[dx - 1])

    def came(at_, send, recv, dy, dx):
        b = peer(-dy, -dx)
        return remote(at_(b), at_(b), send.at[dy, dx], recv.at[dy, dx], (row, peer(dy, dx)))

    g_all, n_all = (g_at, g_s, g_r), (n_at, n_s, n_r)

    def onward(ref):
        for a in range(1, 4):
            came(*ref, a, 0).wait_recv()
            for b in range(1, 4):
                passed(*ref, a, b).start()

    def arrived(ref):
        for a in range(4):
            for b in range(1, 4):
                came(*ref, a, b).wait_recv()

    for c in own(*g_all):
        c.start()
    for c in fetch[1:6]:
        c.wait()
    gain, bias = ln_gain[...].reshape(1, D), ln_bias[...].reshape(1, D)
    b_row = b_up[...].reshape(1, HID)
    for g in range(SUB):
        kflat[pl.ds(g, 49, stride=16)] = kern[:, g * LANE : (g + 1) * LANE]
    for i in range(ROWS):
        for j in range(COLS):
            flat[pl.ds((i * COLS + j) * 16, SUB)] = feat[i, j].astype(F32)
    feat2[...] = jnp.zeros_like(feat2)
    for g in range(SUB):
        feat2[pl.ds(0, PIX), pl.ds(g * LANE, LANE)] = flat[pl.ds(g, PIX, stride=16)]
    for c in f_halo:
        c.wait_recv()
    onward(g_all)
    widen(pad, wide, row, col)

    def line(i, _):
        acc = row_of_taps(wide, kflat, i, False)
        for j in range(COLS):
            flat[pl.ds(pl.multiple_of((i * COLS + j) * 16, 16), SUB)] = acc[j]
        return 0

    lax.fori_loop(0, ROWS, line, 0)
    for g in range(SUB):
        mixed[:, pl.ds(g * LANE, LANE)] = flat[pl.ds(g, PIX, stride=16)]
    m = mixed[...]
    centred = m - jnp.mean(m, axis=-1, keepdims=True)
    var = jnp.mean(centred * centred, axis=-1, keepdims=True)
    normed[col] = (centred * lax.rsqrt(var + 1e-06) * gain + bias).astype(BF16)
    for c in own(*n_all):
        c.start()
    onward(n_all)

    arrived(g_all)
    slots_row = name.astype(F32)
    names = jnp.zeros((SLOT_PAD, 256), F32)
    for d in range(N_COL):
        names = names + every[pl.ds(d * SLOT_PAD, SLOT_PAD), pl.ds(0, 256)].astype(F32)
    names = names[SLOTS : SLOTS + 1] - 1.0

    def token_of(count, first):
        p = lax.broadcasted_iota(jnp.int32, (count, 1), 0)
        d = jnp.where(p >= PIX, 1, 0)
        p = p - d * PIX
        one = lambda c: jnp.where(c, 1, 0)
        i = one(p >= 6) + one(p >= 12) + one(p >= 18)
        j = p - i * COLS
        t = 3 * one(i >= 2) + one(j >= 2) + one(j >= 4)
        return ((first + d) * 6 + t).astype(F32)

    for d in range(0, N_COL, 2):
        hit = token_of(2 * PIX, d) == names
        select[pl.ds(d * PIX, 2 * PIX)] = jnp.where(hit, 1.0, 0.0).astype(BF16)
    p32 = lax.broadcasted_iota(jnp.int32, (32, 1), 0)
    hit = jnp.where(p32 < PIX, token_of(32, col), -9.0) == names
    mine = jnp.where(hit, 1.0, 0.0).astype(BF16)

    def grads(c, _):
        cut = pl.ds(pl.multiple_of(c * 512, 512), 512)
        g = dot(select[...], every[:, cut], 1, 0) * 0.25
        bg[:, cut] = (g * layer_scale[cut].reshape(1, 512)).astype(BF16)
        og[:, cut] = dot(mine, every[:, cut], 1, 0) * 0.25
        return 0

    for c in fetch[6:]:
        c.wait()
    lax.fori_loop(0, 3, grads, 0)

    def hidden_grads(r, _):
        cut = pl.ds(pl.multiple_of(r * 128, 128), 128)
        act_grad[cut] = dot(bg[cut], w_down[...], 1, 1)
        return 0

    lax.fori_loop(0, 3, hidden_grads, 0)

    arrived(n_all)
    for d in range(0, N_COL, 2):
        two = jnp.concatenate([normed[d].astype(F32), normed[d + 1].astype(F32)], axis=0)
        band[pl.ds(d * PIX, 2 * PIX)] = two.astype(BF16)

    def hidden(r, _):
        cut = pl.ds(pl.multiple_of(r * 128, 128), 128)
        v = dot(band[cut], w_up[...], 1, 0) + b_row
        k0, k1 = 0.7978845608028654, 0.044715
        t = jnp.tanh(k0 * (v + k1 * v * v * v))
        act[cut] = (0.5 * v * (1.0 + t)).astype(BF16)
        slope = 0.5 * (1.0 + t) + 0.5 * v * (1.0 - t * t) * (k0 * (1.0 + 3.0 * k1 * v * v))
        pre_grad[cut] = (act_grad[cut] * slope).astype(BF16)
        return 0

    lax.fori_loop(0, 3, hidden, 0)

    def back(c, _):
        cut = pl.ds(pl.multiple_of(c * 512, 512), 512)
        v = dot(pre_grad[...], w_up[cut], 1, 1)
        for d in range(N_COL):
            ng[d, :, cut] = v[d * PIX : (d + 1) * PIX].astype(BF16)
        return 0

    lax.fori_loop(0, 3, back, 0)

    def across_x(at_, to, send, recv):
        out = {}
        for dy in (1, 2, 3, 0):
            for dx in range(1, NX):
                out[dy, dx] = remote(
                    at_(peer(dy, dx)), to.at[dx - 1, dy], send.at[dx, dy], recv.at[dx, dy],
                    xp[dx - 1],
                )
        return out

    def along_y(at_, xs, came_x, held, to, send, recv):
        out = []
        for dy in range(1, NY):
            v = at_(peer(dy, 0))[...].astype(F32)
            for dx in range(1, NX):
                xs[dy, dx].wait_recv()
                v = v + came_x[dx - 1, dy].astype(F32)
            held[dy - 1] = v.astype(BF16)
            out.append(
                remote(held.at[dy - 1], to.at[dy - 1], send.at[dy - 1], recv.at[dy - 1], yp[dy - 1])
            )
            out[-1].start()
        return out

    def at_home(at_, xs, came_x, ys, came_y):
        v = at_(col)[...].astype(F32)
        for dx in range(1, NX):
            xs[0, dx].wait_recv()
            v = v + came_x[dx - 1, 0].astype(F32)
        for dy in range(1, NY):
            ys[dy - 1].wait_recv()
            v = v + came_y[dy - 1].astype(F32)
        return v

    ng_at = lambda d: ng.at[d]
    ng_xs = across_x(ng_at, ng_x, nx_s, nx_r)
    for c in ng_xs.values():
        c.start()

    def down_part(c, _):
        cut = pl.ds(pl.multiple_of(c * 512, 512), 512)
        v = dot(act[...], bg[:, cut], 0, 0)
        for k in range(NC * NZ):
            down[k // NZ, k % NZ, :, cut] = v[k * 16 : (k + 1) * 16].astype(BF16)
        return 0

    lax.fori_loop(0, 3, down_part, 0)
    pair = [
        remote(down.at[1 - core], down0, c_s.at[0], c_r.at[0], twin),
        remote(up.at[1 - core], up0, c_s.at[1], c_r.at[1], twin),
    ]
    pair[0].start()
    for c in range(4):
        v = dot(band[:, c * 384 : (c + 1) * 384], pre_grad[...], 0, 0)
        for k in range(8):
            up[c // 2, c % 2, k] = v[k * 48 : (k + 1) * 48].astype(BF16)
    pair[1].start()

    pooled = (dot(select[...], act[...], 0, 0) * 0.25).astype(BF16)

    def tokens(c, _):
        cut = pl.ds(pl.multiple_of(c * 512, 512), 512)
        v = dot(pooled, w_down[:, cut], 1, 0) * layer_scale[cut].reshape(1, 512)
        v = v + 0.25 * dot(mine, feat2[:, cut].astype(BF16), 0, 0)
        part[:, cut] = v.astype(BF16)
        return 0

    lax.fori_loop(0, 3, tokens, 0)
    part_at = lambda d: part.at[slot_rows(d)]
    part_xs = across_x(part_at, part_x, px_s, px_r)

    for c in pair:
        c.wait_recv()
    for k in range(NZ):
        down_h[k] = (down[core, k].astype(F32) + down0[k].astype(F32)).astype(BF16)
        for n in range(2):
            up_h[n, k] = (up[core, n, k].astype(F32) + up0[n, k].astype(F32)).astype(BF16)
    up_far = remote(up_h.at[1 - yh], up1, h_s.at[0], h_r.at[0], far)
    up_far.start()
    down_z = [
        remote(down_h.at[zb[k]], down1.at[k], dz_s.at[k], dz_r.at[k], zp[k]) for k in range(NZ - 1)
    ]
    for c in down_z:
        c.start()

    ng_ys = along_y(ng_at, ng_xs, ng_x, ng_t, ng_y, ny_s, ny_r)
    for c in part_xs.values():
        c.start()
    total = at_home(ng_at, ng_xs, ng_x, ng_ys, ng_y)
    m = mixed[...]
    centred = m - jnp.mean(m, axis=-1, keepdims=True)
    inv = lax.rsqrt(jnp.mean(centred * centred, axis=-1, keepdims=True) + 1e-06)
    hat = centred * inv
    dy_ = total * gain
    dm = inv * (
        dy_
        - jnp.mean(dy_, axis=-1, keepdims=True)
        - hat * jnp.mean(dy_ * hat, axis=-1, keepdims=True)
    )
    dm = dm.astype(BF16).astype(F32)
    for g in range(SUB):
        flat[pl.ds(g, PIX, stride=16)] = dm[:, g * LANE : (g + 1) * LANE]
    for i in range(ROWS):
        for j in range(COLS):
            v = flat[pl.ds((i * COLS + j) * 16, SUB)]
            mgpad[3 + i, 3 + j] = v.astype(BF16)
            mwide[i, j] = v
    halo = halo_copies(mgpad, row, col, halo_s, halo_r)
    for c in halo:
        c.start()

    def taps(p, _):
        acc = [jnp.zeros((SUB, LANE), F32) for _ in range(7)]
        for i in range(ROWS):
            line = wide[i + p]
            own_line = mwide[i]
            for q in range(7):
                acc[q] = acc[q] + jnp.sum(line[q : q + COLS] * own_line, axis=0)
        for q in range(7):
            t = p * 7 + q
            ker[lax.rem(t, 2), t // 4, lax.rem(t // 2, 2)] = acc[q].astype(BF16)
        return 0

    lax.fori_loop(0, 7, taps, 0)
    for t in range(49, 64):
        ker[t % 2, t // 4, t // 2 % 2] = jnp.zeros((SUB, LANE), BF16)
    k0 = remote(ker.at[1 - core], ker_p, k0_s.at[0], k0_r.at[0], twin)
    k0.start()

    k0.wait_recv()
    for k in range(16):
        ker_h[k] = (ker[core, k].astype(F32) + ker_p[k].astype(F32)).astype(BF16)
    k1 = [
        remote(ker_h.at[colb[k]], ker_in.at[k], k1_s.at[k], k1_r.at[k], colp[k])
        for k in range(N_COL - 1)
    ]
    for c in k1:
        c.start()
    for c in down_z:
        c.wait_recv()
    v = down_h[z].astype(F32)
    for k in range(NZ - 1):
        v = v + down1[k].astype(F32)
    down_c[...] = v.astype(BF16)
    down_far = remote(down_c, down2, h_s.at[1], h_r.at[1], far)
    down_far.start()
    up_far.wait_recv()
    for k in range(NZ):
        up_q[k] = (up_h[yh, k].astype(F32) + up1[k].astype(F32)).astype(BF16)
    up_z = [
        remote(up_q.at[zb[k]], up2.at[k], uz_s.at[k], uz_r.at[k], zp[k]) for k in range(NZ - 1)
    ]
    for c in up_z:
        c.start()

    part_ys = along_y(part_at, part_xs, part_x, part_t, part_y, py_s, py_r)

    for c in k1:
        c.wait_recv()
    v = ker_h[col].astype(F32)
    for k in range(N_COL - 1):
        v = v + ker_in[k].astype(F32)
    ker_z[...] = v.astype(BF16)
    place = yh * NZ + z
    ker_z_in[place] = ker_z[...]
    k2 = [
        remote(ker_z, ker_z_in.at[place], k2_s.at[k], k2_r.at[k], rowp[k]) for k in range(15)
    ]
    for c in k2:
        c.start()

    def up_home(k):
        return lax.rem(z - k + NZ, NZ)

    down_far.wait_recv()
    gdown[core, z] = (down_c[...].astype(F32) + down2[...].astype(F32)).astype(BF16)

    def down_to(where, cc, zz, send, recv):
        ref = gdown.at[cc, zz]
        return remote(ref, ref, send, recv, where)

    da = [down_to(zp[k], core, z, da_s.at[k], da_r.at[k]) for k in range(NZ - 1)]
    dt = [down_to(twin, core, up_home(k), dt_s.at[k], dt_r.at[k]) for k in range(NZ)]
    for c in da:
        c.start()
    dt[0].start()

    for c in halo:
        c.wait_recv()
    widen(mgpad, wide, row, col)
    for g in range(SUB):
        flat[pl.ds(g, PIX, stride=16)] = og[pl.ds(0, PIX), pl.ds(g * LANE, LANE)]

    def line_back(i, _):
        v = row_of_taps(wide, kflat, i, True)
        for j in range(COLS):
            first = flat[pl.ds(pl.multiple_of((i * COLS + j) * 16, 16), SUB)]
            gin[i, j] = (v[j] + first).astype(BF16)
        return 0

    lax.fori_loop(0, ROWS, line_back, 0)

    for c in up_z:
        c.wait_recv()
    v = up_q[z].astype(F32)
    for k in range(NZ - 1):
        v = v + up2[k].astype(F32)
    gup[core, yh, z] = v.astype(BF16)

    def up_to(where, cc, hh, zz, send, recv):
        ref = gup.at[cc, hh, zz]
        return remote(ref, ref, send, recv, where)

    ua = [up_to(zp[k], core, yh, z, ua_s.at[k], ua_r.at[k]) for k in range(NZ - 1)]
    uf = [up_to(far, core, yh, up_home(k), uf_s.at[k], uf_r.at[k]) for k in range(NZ)]
    ut = [up_to(twin, core, yh, up_home(k), ut_s.at[0, k], ut_r.at[0, k]) for k in range(NZ)]
    vt = [up_to(twin, core, 1 - yh, up_home(k), ut_s.at[1, k], ut_r.at[1, k]) for k in range(NZ)]
    for c in ua:
        c.start()
    uf[0].start()
    ut[0].start()
    for k in range(15):
        k2[k].wait_recv()
    v = ker_z_in[0].astype(F32)
    for k in range(1, 16):
        v = v + ker_z_in[k].astype(F32)
    ker_out[core, col] = v.astype(BF16)
    k4 = [
        remote(ker_out.at[core, col], ker_out.at[core, col], k4_s.at[k], k4_r.at[k], colp[k])
        for k in range(N_COL - 1)
    ]
    for c in k4:
        c.start()

    tok = at_home(part_at, part_xs, part_x, part_ys, part_y)
    lanes = lax.broadcasted_iota(jnp.int32, (SLOT_PAD, 256), 1)
    rows = lax.broadcasted_iota(jnp.int32, (SLOT_PAD, 256), 0)
    named = slots_row
    live = jnp.sum(jnp.where(lanes == rows + col * SLOT_PAD, named, 0.0), axis=1, keepdims=True)
    seq[...] = jnp.where(
        live[:SLOTS] > 0.5, tok[:SLOTS].astype(BF16).astype(F32), text[...].astype(F32)
    ).astype(BF16)

    for k in (1, 7, 2, 6, 3, 5, 4):
        b = up_home(k)
        up_to(zp[k - 1], core, yh, b, ua_s.at[k - 1], ua_r.at[k - 1]).wait_recv()
        uf[k].start()
        ut[k].start()
    for k in range(N_COL - 1):
        b = ker_out.at[core, colf[k]]
        remote(b, b, k4_s.at[k], k4_r.at[k], colp[k]).wait_recv()
    k5 = remote(ker_out.at[core], ker_out.at[core], k5_s.at[0], k5_r.at[0], twin)
    k5.start()
    for k in range(1, NZ):
        b = up_home(k)
        down_to(zp[k - 1], core, b, da_s.at[k - 1], da_r.at[k - 1]).wait_recv()
        dt[k].start()
    b = ker_out.at[1 - core]
    remote(b, b, k5_s.at[0], k5_r.at[0], twin).wait_recv()
    for t in range(49):
        kflat[pl.ds(t * 16, SUB)] = ker_out[t % 2, t // 4, t // 2 % 2].astype(F32)
    for g in range(SUB):
        gker[:, g * LANE : (g + 1) * LANE] = kflat[pl.ds(g, 49, stride=16)]
    for k in (0, 1, 7, 2, 6, 3, 5, 4):
        up_to(far, core, 1 - yh, up_home(k), uf_s.at[k], uf_r.at[k]).wait_recv()
        vt[k].start()
    for k in range(NZ):
        b = up_home(k)
        up_to(twin, 1 - core, yh, b, ut_s.at[0, k], ut_r.at[0, k]).wait_recv()
        up_to(twin, 1 - core, 1 - yh, b, ut_s.at[1, k], ut_r.at[1, k]).wait_recv()
        down_to(twin, 1 - core, b, dt_s.at[k], dt_r.at[k]).wait_recv()
    for ref in (g_all, n_all):
        for c in own(*ref):
            c.wait_send()
        for dy in range(1, NY):
            for dx in range(1, NX):
                passed(*ref, dy, dx).wait_send()
    for c in f_halo + list(ng_xs.values()) + list(part_xs.values()) + ng_ys + part_ys + pair:
        c.wait_send()
    for c in halo + [up_far, down_far, k0, k5] + down_z + up_z + k1 + k2 + k4:
        c.wait_send()
    for c in ua + uf + ut + vt + da + dt:
        c.wait_send()


def whole(*operands):
    vm = pl.BlockSpec(memory_space=pltpu.VMEM)
    dma = pltpu.SemaphoreType.DMA
    v = pltpu.VMEM
    w = D // NZ // NC // 2
    h = HID // NZ // NC
    band = N_COL * PIX
    every = N_COL * SLOT_PAD
    map_ = (ROWS + 6, COLS + 6, SUB, LANE)
    return pl.pallas_call(
        whole_kernel,
        out_shape=(
            jax.ShapeDtypeStruct((SLOTS, D), BF16),
            jax.ShapeDtypeStruct((ROWS, COLS, SUB, LANE), BF16),
            jax.ShapeDtypeStruct((49, D), F32),
            jax.ShapeDtypeStruct((NC, 2, NZ, w, HID), BF16),
            jax.ShapeDtypeStruct((NC, NZ, h, D), BF16),
        ),
        in_specs=[vm, pl.BlockSpec(memory_space=pltpu.SMEM)]
        + [pl.BlockSpec(memory_space=pltpu.HBM)] * 9,
        out_specs=[vm] * 5,
        scratch_shapes=[
            v((SLOTS, D), BF16), v((49, D), F32), v((D,), F32), v((D,), F32), v((HID,), F32),
            v((D,), F32), v((HID, D), BF16), v((D, HID), BF16), v((SLOTS, D), BF16),
            v((SLOT_PAD, D), F32),
            v(map_, BF16), v(map_, F32), v((PIX * 16, LANE), F32), v((49 * 16, LANE), F32),
            v((32, D), F32), v((PIX, D), F32),
            v((N_COL, PIX, D), BF16), v((band, D), BF16), v((every, D), BF16),
            v((band, every), BF16), v((band, D), BF16), v((32, D), F32),
            v((band, HID), F32), v((band, HID), BF16), v((band, HID), BF16),
            v((N_COL, PIX, D), BF16), v((NX - 1, NY, PIX, D), BF16),
            v((NY - 1, PIX, D), BF16), v((NY - 1, PIX, D), BF16),
            v((every, D), BF16), v((NX - 1, NY, SLOT_PAD, D), BF16),
            v((NY - 1, SLOT_PAD, D), BF16), v((NY - 1, SLOT_PAD, D), BF16),
            v((NC, 2, NZ, w, HID), BF16), v((NC, NZ, h, D), BF16),
            v((2, NZ, w, HID), BF16), v((NZ, h, D), BF16),
            v((NZ, w, HID), BF16), v((NZ - 1, h, D), BF16),
            v((NZ - 1, w, HID), BF16), v((h, D), BF16),
            v((2, NZ, w, HID), BF16), v((NZ, h, D), BF16),
            v((NZ, w, HID), BF16), v((h, D), BF16),
            v(map_, BF16), v((ROWS, COLS, SUB, LANE), F32),
            v((NC, 16, 2, SUB, LANE), BF16), v((16, 2, SUB, LANE), BF16),
            v((16, 2, SUB, LANE), BF16), v((15, 2, SUB, LANE), BF16),
            v((2, SUB, LANE), BF16), v((16, 2, SUB, LANE), BF16), v((NC, 16, 2, SUB, LANE), BF16),
            dma((9,)), dma((8,)), dma((8,)),
            dma((NY, NX)), dma((NY, NX)), dma((NY, NX)), dma((NY, NX)),
            dma((NX, NY)), dma((NX, NY)), dma((3,)), dma((3,)),
            dma((NX, NY)), dma((NX, NY)), dma((3,)), dma((3,)),
            dma((8,)), dma((8,)),
            dma((2,)), dma((2,)), dma((7,)), dma((7,)), dma((7,)), dma((7,)), dma((2,)), dma((2,)),
            dma((7,)), dma((7,)), dma((7,)), dma((7,)), dma((8,)), dma((8,)), dma((8,)), dma((8,)),
            dma((2, 8)), dma((2, 8)),
            dma((1,)), dma((1,)), dma((15,)), dma((15,)), dma((15,)), dma((15,)),
            dma((15,)), dma((15,)), dma((1,)), dma((1,)),
        ],
        compiler_params=pltpu.CompilerParams(
            collective_id=0, has_side_effects=True, vmem_limit_bytes=VMEM_LIMIT
        ),
    )(*operands)


def local(
    features, kernel, ln_gain, ln_bias, w_up, b_up, w_down, layer_scale,
    text_embed, slot_token, seq_grad,
):
    feat = features.reshape(ROWS, COLS, SUB, LANE)
    seq, gin, gker, gup, gdown = whole(
        feat, slot_token, seq_grad, kernel, ln_gain, ln_bias, b_up, layer_scale, w_down, w_up,
        text_embed,
    )
    return (
        seq, gin.reshape(ROWS, COLS, D), gker, gup.reshape(D, HID), gdown.reshape(HID, D),
    )


def solution(mesh):
    placed = (
        P("row", "col", None), P(), P(), P(), P(None, "col"), P("col"), P("col", None), P(),
        P(("row", "col"), None), P(("row", "col")), P(("row", "col"), None),
    )
    return jax.shard_map(
        local,
        mesh=mesh,
        in_specs=placed,
        out_specs=(
            P(("row", "col"), None), P("row", "col", None), P(), P(None, "col"), P("col", None),
        ),
        check_vma=False,
    )
```
